128 devices in a mesh: img: 8 (over z, y_hi), txt: 16 (over y_lo, x, core).
Axes of the slice: x: 4, y: 4 (y_hi: 2, y_lo: 2; y = y_hi * 2 + y_lo), z: 4, core: 2. Of those that a mesh axis runs over, the one named last changes fastest.
Arguments:
- image_emb: bfloat16 [16384, 1152], P(('img', 'txt')), may hold values from -0.19921875 to 0.19921875
- text_emb: bfloat16 [16384, 1152], P(('txt', 'img')), may hold values from -0.19921875 to 0.19921875
- positive: int32 [16384], P('img'), may hold values from 0 to 16383, each once
- log_scale: float32 [], replicated, may hold values from 1.5 to 2.5
- bias: float32 [], replicated, may hold values from -10 to -6
Outputs:
- loss: float32 [], replicated
- image_grad: float32 [16384, 1152], P(('img', 'txt'))
- text_grad: float32 [16384, 1152], P(('txt', 'img'))
- scale_grad: float32 [], replicated
- bias_grad: float32 [], replicated
The draws below stay inside these ranges and needn't reach their ends.
Inputs may be any that keep to these rules, and one draw needn't show every extreme that they name: Each text row is the positive of exactly one image row.
All inputs are finite; a program needn't handle non-finite values.
Results may differ from the reference program's by a relative error of at most 0.0042.
Values may be sent and summed in bfloat16 or wider, within the bound.
A program may use at most 128 MiB of HBM per device.

```python
import math
import jax
import jax.numpy as jnp
from jax import lax

D = 1152
N = 16384


def block_levels(rng, dims, cuts, least, high):
    level, own = 1.0, jax.random.fold_in(rng, 6)
    for position, shards_of in cuts:
        steps = jnp.exp(jax.random.uniform(jax.random.fold_in(own, position), (shards_of,), jnp.float32, least / len(cuts), high / len(cuts)))
        level = level * jnp.repeat(steps, dims[position] // shards_of).reshape([-1 if axis == position else 1 for axis in range(len(dims))])
    return level


def gaussian(stream_key, extent, spread, bound, pieces=(), held_as=jnp.bfloat16):
    array = spread * jax.random.normal(stream_key, extent, jnp.float32)
    if pieces:
        array = array * block_levels(stream_key, extent, pieces, -0.22, 0.18)
    return jnp.clip(array, -bound, bound).astype(held_as)


def setup_inputs(seed: int = 0) -> dict:
    key_list = jax.random.split(jax.random.key(seed), 6)
    image_emb = gaussian(key_list[0], (N, D), 0.03, 0.19921875, ((0, 128),))
    text_emb = gaussian(key_list[1], (N, D), 0.03, 0.19921875, ((0, 128),))
    positive = jax.random.permutation(key_list[2], N).astype(jnp.int32)
    log_scale = jnp.clip(jax.random.uniform(key_list[3], (), jnp.float32, 1.5, 2.5), 1.5, 2.5)
    bias = jnp.clip(jax.random.uniform(key_list[4], (), jnp.float32, -10.0, -6.0), -10.0, -6.0)
    return {"image_emb": image_emb, "text_emb": text_emb, "positive": positive, "log_scale": log_scale, "bias": bias}


EPS = 1e-06

def unit_rows(emb):
    values = emb.astype(jnp.float32)
    norm = jnp.sqrt(lax.optimization_barrier(jnp.sum(values * values, axis=1, keepdims=True)) + EPS)
    return (values / norm, norm)

def reference(image_emb, text_emb, positive, log_scale, bias):
    image_unit, image_norm = unit_rows(image_emb)
    text_unit, text_norm = unit_rows(text_emb)
    image_low = image_unit.astype(jnp.bfloat16)
    text_low = text_unit.astype(jnp.bfloat16)
    scale = jnp.exp(log_scale)
    columns = jnp.arange(N, dtype=jnp.int32)
    block = math.gcd(N, 512)
    count = N // block

    def step(carry, inputs):
        text_acc, loss_acc, weight_acc, cos_acc = carry
        rows_low, rows_pos = inputs
        cosine = lax.dot_general(rows_low, text_low, (((1,), (1,)), ((), ())), preferred_element_type=jnp.float32)
        logit = scale * cosine + bias
        sign = jnp.where(rows_pos[:, None] == columns[None, :], 1.0, -1.0).astype(jnp.float32)
        margin = -sign * logit
        weight = -sign * jax.nn.sigmoid(margin)
        weight_low = weight.astype(jnp.bfloat16)
        image_part = jnp.dot(weight_low, text_low, preferred_element_type=jnp.float32)
        text_acc = text_acc + lax.dot_general(weight_low, rows_low, (((0,), (0,)), ((), ())), preferred_element_type=jnp.float32)
        carry = (text_acc, loss_acc + jnp.sum(jax.nn.softplus(margin)), weight_acc + jnp.sum(weight), cos_acc + jnp.sum(weight * cosine))
        return (carry, image_part)
    start = (jnp.zeros((N, D), jnp.float32), jnp.zeros((), jnp.float32), jnp.zeros((), jnp.float32), jnp.zeros((), jnp.float32))
    inputs = (image_low.reshape(count, block, D), positive.reshape(count, block))
    (text_acc, loss_sum, weight_sum, cos_sum), image_parts = lax.scan(step, start, inputs)
    unit_image_grad = scale * image_parts.reshape(N, D)
    unit_text_grad = scale * text_acc
    image_grad = (unit_image_grad - image_unit * lax.optimization_barrier(jnp.sum(image_unit * unit_image_grad, axis=1, keepdims=True))) / image_norm
    text_grad = (unit_text_grad - text_unit * lax.optimization_barrier(jnp.sum(text_unit * unit_text_grad, axis=1, keepdims=True))) / text_norm
    return (loss_sum / N, image_grad, text_grad, scale * cos_sum, weight_sum)
```

```python
import jax
import jax.numpy as jnp
from jax import lax
from jax.experimental import pallas as pl
from jax.experimental.pallas import tpu as pltpu
from jax.sharding import PartitionSpec as P

EPS = 1e-06
LOG2E = 1.4426950408889634
MESH = pl.DeviceIdType.MESH
OWN, PAIR = 0, 1
ROWS = 128
HALF = ROWS // 2
PLUS, MINUS = 0, 1

NAMES = []
for _kind in ("image", "text"):
    NAMES += [(_kind, "y", h) for h in (0, 1)]
    NAMES += [(_kind, step, way, h) for step in ("own", "pair") for way in (PLUS, MINUS) for h in (0, 1)]
    NAMES += [(_kind, step, way) for step in ("own2", "pair2") for way in (PLUS, MINUS)]
    NAMES += [(_kind, "far", way, t) for way in (PLUS, MINUS) for t in (OWN, PAIR)]
    NAMES += [(_kind, "near", way, t) for way in (PLUS, MINUS) for t in (OWN, PAIR)]
    NAMES += [(_kind, "home")]
NAMES += [("core", t, d) for t in (OWN, PAIR) for d in range(4)]
NAMES += [("coresum", t, d) for t in (OWN, PAIR) for d in range(4)]
NAMES += [("sum", stage) for stage in ("core", "y", "yy")]
NAMES += [("sum", axis, d) for axis in ("x", "z") for d in (1, 2, 3)]
IDS = {name: i for i, name in enumerate(NAMES)}


def unit_rows(emb):
    values = emb.astype(jnp.float32)
    norm = jnp.sqrt(jnp.sum(values * values, axis=1, keepdims=True) + EPS)
    return values / norm, norm


class Ring:
    def __init__(self, kind, rows, partner, plus, minus, slot):
        self.kind, self.rows, self.partner = kind, rows, partner
        self.to = {PLUS: plus, MINUS: minus}
        self.slot = slot

    def part(self, t, d, h):
        return self.rows.at[pl.ds(pl.multiple_of(self.slot(t, d) * ROWS + h * HALF, HALF), HALF)]


def kernel(
    image_emb, text_emb, positive, log_scale, bias,
    loss_ref, image_grad, text_grad, scale_grad, bias_grad,
    image_rows, text_rows, weight, weight_t, image_unit, text_unit, image_norm, text_norm,
    image_own, text_own, core_out, core_in,
    image_far_out, image_far_in, image_near_out, image_near_in, image_home_out, image_home_in,
    text_far_out, text_far_in, text_near_out, text_near_in, text_home_out, text_home_in,
    totals, sums, sums_in, ring_sums, send_sem, recv_sem,
):
    img, txt = lax.axis_index("img"), lax.axis_index("txt")
    z, yh = lax.div(img, 2), lax.rem(img, 2)
    yl, x, c = lax.div(txt, 8), lax.rem(lax.div(txt, 2), 4), lax.rem(txt, 2)

    def device(z=z, yh=yh, yl=yl, x=x, c=c):
        return (z * 2 + yh, yl * 8 + x * 2 + c)

    def step(i, d):
        return lax.rem(i + d, 4)

    sibling = device(c=1 - c)
    image_partner = device(yl=1 - yl)
    text_partner = device(yl=1 - yl, yh=1 - yh)
    x_at = {d: device(x=step(x, d)) for d in (1, 2, 3)}
    z_at = {d: device(z=step(z, d)) for d in (1, 2, 3)}

    barrier = pltpu.get_barrier_semaphore()
    partners = [sibling, image_partner, text_partner, *x_at.values(), *z_at.values()]
    for partner in partners:
        pl.semaphore_signal(barrier, inc=1, device_id=partner, device_id_type=MESH)

    def image_slot(t, d, core=c):
        return (yl + t * (1 - 2 * yl)) * 8 + step(x, d) * 2 + core

    def text_slot(t, d):
        return step(z, d) * 2 + (yh + t * (1 - 2 * yh))

    image = Ring("image", image_rows, image_partner, x_at[1], x_at[3], image_slot)
    text = Ring("text", text_rows, text_partner, z_at[1], z_at[3], text_slot)

    started = []

    def send(name, src, dst, to):
        i = IDS[name]
        copy = pltpu.make_async_remote_copy(
            src_ref=src, dst_ref=dst, send_sem=send_sem.at[i], recv_sem=recv_sem.at[i], device_id=to, device_id_type=MESH
        )
        copy.start()
        started.append(copy)

    def recv(name, dst):
        i = IDS[name]
        pltpu.make_async_remote_copy(
            src_ref=dst, dst_ref=dst, send_sem=send_sem.at[i], recv_sem=recv_sem.at[i], device_id=sibling, device_id_type=MESH
        ).wait_recv()

    def block(slot):
        return pl.ds(pl.multiple_of(slot * ROWS, ROWS), ROWS)

    def own_rows(emb, ring, unit_ref, norm_ref):
        unit, norm = unit_rows(emb[...])
        unit_ref[...] = unit
        norm_ref[...] = norm
        ring.rows[block(ring.slot(OWN, 0)), :] = unit.astype(jnp.bfloat16)

    own_rows(image_emb, image, image_unit, image_norm)
    own_rows(text_emb, text, text_unit, text_norm)
    pl.semaphore_wait(barrier, len(partners))

    def forward(ring, name, t, d, h, to):
        part = ring.part(t, d, h)
        send((ring.kind, *name), part, part, to)

    def arrived(ring, name, t, d, h):
        recv((ring.kind, *name), ring.part(t, d, h))

    def to_sibling(t, d):
        part = image_rows.at[block(image_slot(t, d))]
        send(("core", t, d), part, part, sibling)

    def from_sibling(t, d):
        recv(("core", t, d), image_rows.at[block(image_slot(t, d, 1 - c))])

    def gather_start(ring):
        for h in (0, 1):
            forward(ring, ("y", h), OWN, 0, h, ring.partner)
            forward(ring, ("own", PLUS, h), OWN, 0, h, ring.to[PLUS])
            forward(ring, ("own", MINUS, 1 - h), OWN, 0, 1 - h, ring.to[MINUS])

    def gather_first(ring):
        arrived(ring, ("own", PLUS, 0), OWN, 3, 0)
        forward(ring, ("own2", PLUS), OWN, 3, 0, ring.to[PLUS])
        arrived(ring, ("own", MINUS, 1), OWN, 1, 1)
        forward(ring, ("own2", MINUS), OWN, 1, 1, ring.to[MINUS])
        arrived(ring, ("y", 0), PAIR, 0, 0)
        for way in (PLUS, MINUS):
            forward(ring, ("pair", way, 0), PAIR, 0, 0, ring.to[way])

    def gather_second(ring):
        arrived(ring, ("y", 1), PAIR, 0, 1)
        for way in (PLUS, MINUS):
            forward(ring, ("pair", way, 1), PAIR, 0, 1, ring.to[way])
        arrived(ring, ("own", PLUS, 1), OWN, 3, 1)
        arrived(ring, ("own", MINUS, 0), OWN, 1, 0)

    def gather_third(ring):
        arrived(ring, ("pair", PLUS, 0), PAIR, 3, 0)
        forward(ring, ("pair2", PLUS), PAIR, 3, 0, ring.to[PLUS])
        arrived(ring, ("pair", MINUS, 1), PAIR, 1, 1)
        forward(ring, ("pair2", MINUS), PAIR, 1, 1, ring.to[MINUS])
        arrived(ring, ("pair", PLUS, 1), PAIR, 3, 1)
        arrived(ring, ("pair", MINUS, 0), PAIR, 1, 0)

    def gather_last(ring):
        arrived(ring, ("own2", PLUS), OWN, 2, 0)
        arrived(ring, ("own2", MINUS), OWN, 2, 1)
        arrived(ring, ("pair2", PLUS), PAIR, 2, 0)
        arrived(ring, ("pair2", MINUS), PAIR, 2, 1)

    scale = jnp.exp(jnp.full((1, 128), log_scale[0], jnp.float32))
    scale2 = jnp.concatenate([scale * LOG2E] * 2, axis=1)
    bias2 = jnp.full((1, 256), bias[0] * LOG2E, jnp.float32)
    totals[...] = jnp.zeros_like(totals)

    def fold(values):
        return values[:, :128] + values[:, 128:]

    def tile(dz, t, dx):
        zt = step(z, dz)
        start = pl.multiple_of(zt * 256, 256)
        columns = pl.multiple_of(image_slot(t, dx, 0) * ROWS, 256)
        cosine = lax.dot_general(
            text_rows[pl.ds(start, 256), :], image_rows[pl.ds(columns, 256), :],
            (((1,), (1,)), ((), ())), preferred_element_type=jnp.float32,
        )
        wanted = positive[:, pl.ds(columns, 256)]
        add = [jnp.zeros((8, 256), jnp.float32) for _ in range(4)]
        for q in (0, 1):
            lo = yl + (q - yh) * (q - yh) * (1 - 2 * yl)
            first = ((lo * 8 + x * 2 + c) * 8 + zt * 2 + q) * ROWS
            for part in (0, 1):
                rows = slice(q * ROWS + part * HALF, q * ROWS + (part + 1) * HALF)
                cos = cosine[rows]
                row = lax.broadcasted_iota(jnp.int32, (HALF, 256), 0)
                hot = (row == wanted - (first + part * HALF)).astype(jnp.float32)
                e = jnp.exp2(cos * scale2 + bias2)
                u = 1.0 + e
                w = e / u - hot
                weight_t[pl.ds(pl.multiple_of(start + rows.start, HALF), HALF), pl.ds(columns, 256)] = w.astype(jnp.bfloat16)
                e8, u8 = e.reshape(8, 8, 256), u.reshape(8, 8, 256)
                product = e8[0]
                for k in range(1, 8):
                    product = product * u8[k] + e8[k]
                add[0] += jnp.log1p(product)
                add[1] += jnp.sum(w.reshape(8, 8, 256), axis=0)
                add[2] += jnp.sum((w * cos).reshape(8, 8, 256), axis=0)
                add[3] += jnp.sum((hot * cos).reshape(8, 8, 256), axis=0)
            at = pl.multiple_of(start + q * ROWS, ROWS)
            weight[pl.ds(columns, 256), pl.ds(at, ROWS)] = weight_t[pl.ds(at, ROWS), pl.ds(columns, 256)].T
        for i in range(4):
            totals[i] += fold(add[i])

    def tiles(count, place):
        def body(i, carry):
            tile(*place(i))
            return carry

        lax.fori_loop(0, count, body, 0)

    def three(i):
        return lax.div(i * (i + 1), 2)

    gather_start(image)
    gather_start(text)
    to_sibling(OWN, 0)
    gather_first(image)
    gather_first(text)
    gather_second(image)
    gather_second(text)
    to_sibling(OWN, 3)
    to_sibling(OWN, 1)
    to_sibling(PAIR, 0)
    for t, d in ((OWN, 0), (OWN, 3), (OWN, 1), (PAIR, 0)):
        from_sibling(t, d)
    tiles(2, lambda i: (0, i, 0))
    tiles(2, lambda i: (0, OWN, 1 + 2 * i))
    gather_third(image)
    gather_third(text)
    to_sibling(PAIR, 3)
    to_sibling(PAIR, 1)
    for d in (3, 1):
        from_sibling(PAIR, d)
    tiles(2, lambda i: (0, PAIR, 1 + 2 * i))
    tiles(12, lambda i: (1 + 2 * lax.div(i, 6), lax.rem(i, 2), three(lax.rem(lax.div(i, 2), 3))))
    gather_last(image)
    to_sibling(OWN, 2)
    to_sibling(PAIR, 2)
    gather_last(text)
    from_sibling(OWN, 2)
    from_sibling(PAIR, 2)
    tiles(8, lambda i: (lax.rem(i, 4), lax.div(i, 4), 2))

    def place(t, d):
        return t * 4 + d

    def image_parts(blocks):
        lhs = []
        for t, d in blocks:
            lhs += [weight[block(image_slot(t, d)), :], weight[block(image_slot(t, d, 1 - c)), :]]
        out = jnp.dot(jnp.concatenate(lhs, axis=0), text_rows[...], preferred_element_type=jnp.float32)
        for n, (t, d) in enumerate(blocks):
            image_own[place(t, d)] = out[n * 256 : n * 256 + ROWS]
            core_out[place(t, d)] = out[n * 256 + ROWS : (n + 1) * 256].astype(jnp.bfloat16)
            send(("coresum", t, d), core_out.at[place(t, d)], core_in.at[place(t, d)], sibling)

    def text_parts(steps):
        blocks = [(t, d) for d in steps for t in (PAIR, OWN)]
        lhs = [weight_t[block(text_slot(t, d)), :] for t, d in blocks]
        out = jnp.dot(jnp.concatenate(lhs, axis=0), image_rows[...], preferred_element_type=jnp.float32)
        for n, (t, d) in enumerate(blocks):
            text_own[place(t, d)] = out[n * ROWS : (n + 1) * ROWS]

    def image_part(t, d):
        recv(("coresum", t, d), core_in.at[place(t, d)])
        return image_own[place(t, d)] + core_in[place(t, d)].astype(jnp.float32)

    def text_part(t, d):
        return text_own[place(t, d)]

    def send_far(ring, part, out, into, t):
        value = part(t, 2).astype(jnp.bfloat16)
        for way in (PLUS, MINUS):
            out[t, way] = value[way * HALF : (way + 1) * HALF]
            send((ring.kind, "far", way, t), out.at[t, way], into.at[t, way], ring.to[way])

    def send_near(ring, part, far_in, out, into, t):
        for way in (PLUS, MINUS):
            value = part(t, 1 if way == PLUS else 3)
            recv((ring.kind, "far", way, t), far_in.at[t, way])
            mine = slice(way * HALF, (way + 1) * HALF)
            other = slice((1 - way) * HALF, (2 - way) * HALF)
            out[t, way, mine] = (value[mine] + far_in[t, way].astype(jnp.float32)).astype(jnp.bfloat16)
            out[t, way, other] = value[other].astype(jnp.bfloat16)
            send((ring.kind, "near", way, t), out.at[t, way], into.at[t, way], ring.to[way])

    def ring_sum(ring, part, near_in, t):
        value = part(t, 0)
        for way in (PLUS, MINUS):
            recv((ring.kind, "near", way, t), near_in.at[t, way])
            value = value + near_in[t, way].astype(jnp.float32)
        return value

    def send_home(ring, part, near_in, out, into):
        out[...] = ring_sum(ring, part, near_in, PAIR).astype(jnp.bfloat16)
        send((ring.kind, "home"), out, into, ring.partner)

    def finish(ring, part, near_in, home_in, unit_ref, norm_ref, grad):
        value = ring_sum(ring, part, near_in, OWN)
        recv((ring.kind, "home"), home_in)
        value = (value + home_in[...].astype(jnp.float32)) * scale[:, :1]
        unit = unit_ref[...]
        grad[...] = (value - unit * jnp.sum(unit * value, axis=1, keepdims=True)) / norm_ref[...]

    image_parts([(PAIR, 2), (OWN, 2)])
    tiles(6, lambda i: (2, lax.rem(i, 2), three(lax.div(i, 2))))
    for t in (PAIR, OWN):
        send_far(image, image_part, image_far_out, image_far_in, t)

    for i in range(4):
        sums[0, i : i + 1] = jnp.sum(totals[i], axis=0, keepdims=True)
    sums[0, 4:] = jnp.zeros((4, 128), jnp.float32)
    send(("sum", "core"), sums.at[0], sums_in.at[0], sibling)

    text_parts([2])
    for t in (PAIR, OWN):
        send_far(text, text_part, text_far_out, text_far_in, t)

    def next_sum(i, name):
        recv(("sum", name), sums_in.at[i])
        sums[i + 1] = sums[i] + sums_in[i]

    next_sum(0, "core")
    send(("sum", "y"), sums.at[1], sums_in.at[1], image_partner)

    image_parts([(PAIR, 1), (PAIR, 3)])
    text_parts([1, 3])
    send_near(image, image_part, image_far_in, image_near_out, image_near_in, PAIR)
    send_near(text, text_part, text_far_in, text_near_out, text_near_in, PAIR)
    next_sum(1, "y")
    send(("sum", "yy"), sums.at[2], sums_in.at[2], text_partner)

    image_parts([(OWN, 1), (OWN, 3)])
    send_near(text, text_part, text_far_in, text_near_out, text_near_in, OWN)
    send_near(image, image_part, image_far_in, image_near_out, image_near_in, OWN)
    next_sum(2, "yy")

    def share(i, axis, me, at, source):
        ring_sums[i, me] = sums[source]
        for d in (1, 2, 3):
            send(("sum", axis, d), sums.at[source], ring_sums.at[i, me], at[d])

    def shared(i, axis, me, into):
        for d in (1, 2, 3):
            recv(("sum", axis, d), ring_sums.at[i, step(me, 4 - d)])
        sums[into] = (ring_sums[i, 0] + ring_sums[i, 1]) + (ring_sums[i, 2] + ring_sums[i, 3])

    share(0, "x", x, x_at, 3)
    image_parts([(PAIR, 0), (OWN, 0)])
    text_parts([0])
    shared(0, "x", x, 4)
    share(1, "z", z, z_at, 4)

    send_home(image, image_part, image_near_in, image_home_out, image_home_in)
    send_home(text, text_part, text_near_in, text_home_out, text_home_in)
    shared(1, "z", z, 5)
    finish(image, image_part, image_near_in, image_home_in, image_unit, image_norm, image_grad)
    finish(text, text_part, text_near_in, text_home_in, text_unit, text_norm, text_grad)

    total = jnp.sum(sums[5], axis=1, keepdims=True)
    pairs = positive.shape[1] * 8
    factor = scale[:, :1]
    loss_ref[...] = (total[0:1] - factor * total[3:4]) / pairs - bias[0]
    scale_grad[...] = factor * total[2:3]
    bias_grad[...] = total[1:2]
    for copy in started:
        copy.wait_send()


def body(image_emb, text_emb, positive, log_scale, bias):
    rows, width = image_emb.shape
    images, texts = 16 * rows, 8 * rows
    low, full = jnp.bfloat16, jnp.float32
    vmem = pl.BlockSpec(memory_space=pltpu.VMEM)
    smem = pl.BlockSpec(memory_space=pltpu.SMEM)
    scalar = jax.ShapeDtypeStruct((1, 1), full)
    grad = jax.ShapeDtypeStruct((rows, width), full)
    sums_home = [
        pltpu.VMEM((2, 2, HALF, width), low), pltpu.VMEM((2, 2, HALF, width), low),
        pltpu.VMEM((2, 2, rows, width), low), pltpu.VMEM((2, 2, rows, width), low),
        pltpu.VMEM((rows, width), low), pltpu.VMEM((rows, width), low),
    ]
    loss, image_grad, text_grad, scale_grad, bias_grad = pl.pallas_call(
        kernel,
        out_shape=(scalar, grad, grad, scalar, scalar),
        in_specs=[vmem, vmem, vmem, smem, smem],
        out_specs=(vmem,) * 5,
        scratch_shapes=[
            pltpu.VMEM((images, width), low),
            pltpu.VMEM((texts, width), low),
            pltpu.VMEM((images, texts), low),
            pltpu.VMEM((texts, images), low),
            pltpu.VMEM((rows, width), full),
            pltpu.VMEM((rows, width), full),
            pltpu.VMEM((rows, 1), full),
            pltpu.VMEM((rows, 1), full),
            pltpu.VMEM((8, rows, width), full),
            pltpu.VMEM((8, rows, width), full),
            pltpu.VMEM((8, rows, width), low),
            pltpu.VMEM((8, rows, width), low),
            *sums_home,
            *sums_home,
            pltpu.VMEM((4, 8, 128), full),
            pltpu.VMEM((6, 8, 128), full),
            pltpu.VMEM((3, 8, 128), full),
            pltpu.VMEM((2, 4, 8, 128), full),
            pltpu.SemaphoreType.DMA((len(NAMES),)),
            pltpu.SemaphoreType.DMA((len(NAMES),)),
        ],
        compiler_params=pltpu.CompilerParams(collective_id=0, has_side_effects=True, vmem_limit_bytes=56 * 2**20),
    )(image_emb, text_emb, positive.reshape(1, images), log_scale.reshape(1), bias.reshape(1))
    return loss.reshape(()), image_grad, text_grad, scale_grad.reshape(()), bias_grad.reshape(())


def solution(mesh):
    placed = (P(("img", "txt"), None), P(("txt", "img"), None), P("img"), P(), P())
    return jax.shard_map(
        body,
        mesh=mesh,
        in_specs=placed,
        out_specs=(P(), P(("img", "txt"), None), P(("txt", "img"), None), P(), P()),
        check_vma=False,
    )
```

```python
import jax
import jax.numpy as jnp
from jax import lax
from jax.experimental import pallas as pl
from jax.experimental.pallas import tpu as pltpu
from jax.sharding import PartitionSpec as P

EPS = 1e-06
LOG2E = 1.4426950408889634
MESH = pl.DeviceIdType.MESH
OWN, PAIR = 0, 1
ROWS = 128
HALF = ROWS // 2
QUARTER = ROWS // 4
PLUS, MINUS = 0, 1
OWN_A, OWN_B, PAIR_A = 0, 1, 2
FIRST = [(OWN, 0), (PAIR, 0), (OWN, 1), (OWN, 3)]
SECOND = [(PAIR, 1), (PAIR, 3), (OWN, 2)]
LAST = [(PAIR, 2)]

NAMES = []
for _kind in ("image", "text"):
    NAMES += [(_kind, "y", h) for h in (0, 1)]
    NAMES += [(_kind, "y_ring", d) for d in (1, 2, 3)]
    NAMES += [(_kind, "own", way, h) for way in (PLUS, MINUS) for h in (0, 1)]
    NAMES += [(_kind, "own2", way, h) for way in (PLUS, MINUS) for h in (0, 1)]
    NAMES += [(_kind, step, way) for step in ("pair", "pair2") for way in (PLUS, MINUS)]
    NAMES += [(_kind, "y_sum", d) for d in range(4)]
    NAMES += [(_kind, step, way, part) for step in ("far", "near") for way in (PLUS, MINUS) for part in range(3)]
    NAMES += [(_kind, "home")]
NAMES += [("core", t, d) for t in (OWN, PAIR) for d in range(4)]
NAMES += [("coresum", t, d) for t in (OWN, PAIR) for d in range(4)]
NAMES += [("sum", stage) for stage in ("core", "y", "yy")]
NAMES += [("sum", axis, d) for axis in ("x", "z") for d in (1, 2, 3)]
IDS = {name: i for i, name in enumerate(NAMES)}


def unit_rows(emb):
    values = emb.astype(jnp.float32)
    norm = jnp.sqrt(jnp.sum(values * values, axis=1, keepdims=True) + EPS)
    return values / norm, norm


class Ring:
    def __init__(self, kind, rows, partner, plus, minus, slot):
        self.kind, self.rows, self.partner = kind, rows, partner
        self.to = {PLUS: plus, MINUS: minus}
        self.slot = slot

    def part(self, t, d, first, count):
        return self.rows.at[pl.ds(pl.multiple_of(self.slot(t, d) * ROWS + first, QUARTER), count)]


class Home:
    def __init__(self, own, far_out, far_in, near_out, near_in, y_out, y_in, home_out, home_in):
        self.own, self.far_out, self.far_in, self.near_out, self.near_in = own, far_out, far_in, near_out, near_in
        self.y_out, self.y_in, self.home_out, self.home_in = y_out, y_in, home_out, home_in


def kernel(
    image_emb, text_emb, positive_in, log_scale, bias,
    image_sum, text_sum, scalar_sums,
    image_in, text_in, positive, image_rows, text_rows, weight_t, core_out, core_in, *rest,
):
    image_home, text_home = Home(*rest[:9]), Home(*rest[9:18])
    totals, sums, sums_in, ring_sums, send_sem, recv_sem, load_sem = rest[18:]
    img, txt = lax.axis_index("img"), lax.axis_index("txt")
    z, yh = lax.div(img, 2), lax.rem(img, 2)
    yl, x, c = lax.div(txt, 8), lax.rem(lax.div(txt, 2), 4), lax.rem(txt, 2)

    loads = [
        pltpu.make_async_copy(src, dst, load_sem.at[i])
        for i, (src, dst) in enumerate(((image_emb, image_in), (text_emb, text_in), (positive_in, positive)))
    ]
    for load in loads:
        load.start()

    def device(z=z, yh=yh, yl=yl, x=x, c=c):
        return (z * 2 + yh, yl * 8 + x * 2 + c)

    def step(i, d):
        return lax.rem(i + d, 4)

    def other(bit, t):
        return bit + t * (1 - 2 * bit)

    sibling = device(c=1 - c)
    image_partner = device(yl=1 - yl)
    text_partner = device(yl=1 - yl, yh=1 - yh)
    x_at = {d: device(x=step(x, d)) for d in (1, 2, 3)}
    z_at = {d: device(z=step(z, d)) for d in (1, 2, 3)}

    barrier = pltpu.get_barrier_semaphore()
    partners = [sibling, image_partner, text_partner, *x_at.values(), *z_at.values()]
    for partner in partners:
        pl.semaphore_signal(barrier, inc=1, device_id=partner, device_id_type=MESH)

    def image_slot(t, d, core=c):
        return other(yl, t) * 8 + step(x, d) * 2 + core

    def text_slot(t, d):
        return step(z, d) * 2 + other(yh, t)

    image = Ring("image", image_rows, image_partner, x_at[1], x_at[3], image_slot)
    text = Ring("text", text_rows, text_partner, z_at[1], z_at[3], text_slot)

    started = []

    def send(name, src, dst, to):
        i = IDS[name]
        copy = pltpu.make_async_remote_copy(
            src_ref=src, dst_ref=dst, send_sem=send_sem.at[i], recv_sem=recv_sem.at[i], device_id=to, device_id_type=MESH
        )
        copy.start()
        started.append(copy)

    def recv(name, dst):
        i = IDS[name]
        pltpu.make_async_remote_copy(
            src_ref=dst, dst_ref=dst, send_sem=send_sem.at[i], recv_sem=recv_sem.at[i], device_id=sibling, device_id_type=MESH
        ).wait_recv()

    def block(slot):
        return pl.ds(pl.multiple_of(slot * ROWS, ROWS), ROWS)

    def own_rows(load, emb, ring):
        load.wait()
        unit, _ = unit_rows(emb[...])
        ring.rows[block(ring.slot(OWN, 0)), :] = unit.astype(jnp.bfloat16)

    own_rows(loads[0], image_in, image)
    own_rows(loads[1], text_in, text)
    pl.semaphore_wait(barrier, len(partners))

    def forward(ring, name, t, d, first, count, to):
        part = ring.part(t, d, first, count)
        send((ring.kind, *name), part, part, to)

    def arrived(ring, name, t, d, first, count):
        recv((ring.kind, *name), ring.part(t, d, first, count))

    def to_sibling(blocks):
        for t, d in blocks:
            part = image_rows.at[block(image_slot(t, d))]
            send(("core", t, d), part, part, sibling)

    def from_sibling(blocks):
        for t, d in blocks:
            recv(("core", t, d), image_rows.at[block(image_slot(t, d, 1 - c))])

    def quarter(way, h):
        return h * HALF + way * QUARTER, QUARTER

    def near(way):
        return 3 if way == PLUS else 1

    def gather_start(ring):
        forward(ring, ("y", 0), OWN, 0, 0, HALF, ring.partner)
        for h in (1, 0):
            for way in (PLUS, MINUS):
                forward(ring, ("own", way, h), OWN, 0, h * HALF, HALF, ring.to[way])
        forward(ring, ("y", 1), OWN, 0, HALF, HALF, ring.partner)

    def gather_ring(ring, h):
        for way in (PLUS, MINUS):
            d = near(way)
            arrived(ring, ("own", way, h), OWN, d, h * HALF, HALF)
            forward(ring, ("own2", way, h), OWN, d, *quarter(way, h), ring.to[way])
            if h == 1:
                forward(ring, ("y_ring", d), OWN, d, HALF, HALF, ring.partner)

    def gather_pair(ring):
        arrived(ring, ("y", 0), PAIR, 0, 0, HALF)
        for way in (PLUS, MINUS):
            forward(ring, ("pair", way), PAIR, 0, 0, HALF, ring.to[way])

    def gather_far(ring):
        for way in (PLUS, MINUS):
            arrived(ring, ("own2", way, 1), OWN, 2, *quarter(way, 1))
        forward(ring, ("y_ring", 2), OWN, 2, HALF, HALF, ring.partner)

    def gather_pair_ring(ring):
        for way in (PLUS, MINUS):
            d = near(way)
            arrived(ring, ("pair", way), PAIR, d, 0, HALF)
            forward(ring, ("pair2", way), PAIR, d, *quarter(way, 0), ring.to[way])

    def gather_second(ring):
        for d in (1, 3):
            arrived(ring, ("y_ring", d), PAIR, d, HALF, HALF)
        for way in (PLUS, MINUS):
            arrived(ring, ("own2", way, 0), OWN, 2, *quarter(way, 0))

    def gather_last(ring):
        arrived(ring, ("y_ring", 2), PAIR, 2, HALF, HALF)
        for way in (PLUS, MINUS):
            arrived(ring, ("pair2", way), PAIR, 2, *quarter(way, 0))

    scale = jnp.exp(jnp.full((1, 256), log_scale[0], jnp.float32))
    scale2 = scale * LOG2E
    bias2 = jnp.full((1, 256), bias[0] * LOG2E, jnp.float32)
    totals[...] = jnp.zeros_like(totals)

    def tile(blocks, t, dx):
        columns = pl.multiple_of(image_slot(t, dx, 0) * ROWS, 256)
        cosine = lax.dot_general(
            jnp.concatenate([text_rows[block(text_slot(*b)), :] for b in blocks], axis=0),
            image_rows[pl.ds(columns, 256), :], (((1,), (1,)), ((), ())), preferred_element_type=jnp.float32,
        )
        wanted = positive[:, pl.ds(columns, 256)]
        add = [jnp.zeros((8, 256), jnp.float32) for _ in range(3)]
        for n, (tt, dz) in enumerate(blocks):
            at = text_slot(tt, dz) * ROWS
            first = ((other(yl, tt) * 8 + x * 2 + c) * 8 + text_slot(tt, dz)) * ROWS
            for part in (0, HALF):
                cos = cosine[n * ROWS + part : n * ROWS + part + HALF]
                row = lax.broadcasted_iota(jnp.int32, (HALF, 256), 0)
                flip = jnp.where(row == wanted - (first + part), -1.0, 1.0)
                e = jnp.exp2((cos * scale2 + bias2) * flip)
                u = 1.0 + e
                w = (e / u) * flip
                weight_t[pl.ds(pl.multiple_of(at + part, HALF), HALF), pl.ds(columns, 256)] = w.astype(jnp.bfloat16)
                e8, u8 = e.reshape(8, 8, 256), u.reshape(8, 8, 256)
                product = e8[0]
                for k in range(1, 8):
                    product = product * u8[k] + e8[k]
                add[0] += jnp.log1p(product)
                add[1] += jnp.sum(w.reshape(8, 8, 256), axis=0)
                add[2] += jnp.sum((w * cos).reshape(8, 8, 256), axis=0)
        for i in range(3):
            totals[i] += add[i][:, :128] + add[i][:, 128:]

    def tiles(blocks, count, place):
        def body(i, carry):
            tile(blocks, *place(i))
            return carry

        lax.fori_loop(0, count, body, 0)

    def first_place(i):
        return lax.rem(i, 2) * (1 - lax.div(i, 2)), lax.div(i * (i - 1), 2)

    def place(t, d):
        return t * 4 + d

    def image_parts(blocks):
        slots = [image_slot(t, d, core) for t, d in blocks for core in (c, 1 - c)]
        lhs = jnp.concatenate([weight_t[:, block(slot)] for slot in slots], axis=1)
        out = lax.dot_general(lhs, text_rows[...], (((0,), (0,)), ((), ())), preferred_element_type=jnp.float32)
        for n, (t, d) in enumerate(blocks):
            core_out[place(t, d)] = out[n * 256 + ROWS : (n + 1) * 256].astype(jnp.bfloat16)
            send(("coresum", t, d), core_out.at[place(t, d)], core_in.at[place(t, d)], sibling)
            image_home.own[place(t, d)] = out[n * 256 : n * 256 + ROWS]

    def text_parts(blocks):
        lhs = jnp.concatenate([weight_t[block(text_slot(t, d)), :] for t, d in blocks], axis=0)
        out = jnp.dot(lhs, image_rows[...], preferred_element_type=jnp.float32)
        for n, (t, d) in enumerate(blocks):
            text_home.own[place(t, d)] = out[n * ROWS : (n + 1) * ROWS]

    def image_ready(blocks):
        for t, d in blocks:
            recv(("coresum", t, d), core_in.at[place(t, d)])

    def image_part(t, d, half):
        rows = slice(half * HALF, (half + 1) * HALF)
        return image_home.own[place(t, d), rows] + core_in[place(t, d), rows].astype(jnp.float32)

    def text_part(t, d, half):
        return text_home.own[place(t, d), half * HALF : (half + 1) * HALF]

    class Sums:
        def __init__(self, ring, home, part):
            self.ring, self.home, self.part = ring, home, part

        def send(self, name, src, dst, to):
            send((self.ring.kind, *name), src, dst, to)

        def recv(self, name, dst):
            recv((self.ring.kind, *name), dst)

        def value(self, part, d):
            if part == OWN_B:
                self.recv(("y_sum", d), self.home.y_in.at[d])
                return self.part(OWN, d, 1) + self.home.y_in[d].astype(jnp.float32)
            return self.part(OWN if part == OWN_A else PAIR, d, 0)

        def send_y(self, d):
            self.home.y_out[d] = self.part(PAIR, d, 1).astype(jnp.bfloat16)
            self.send(("y_sum", d), self.home.y_out.at[d], self.home.y_in.at[d], self.ring.partner)

        def send_far(self, part):
            value = self.value(part, 2).astype(jnp.bfloat16)
            for way in (PLUS, MINUS):
                self.home.far_out[part, way] = value[way * QUARTER : (way + 1) * QUARTER]
                out, into = self.home.far_out.at[part, way], self.home.far_in.at[part, way]
                self.send(("far", way, part), out, into, self.ring.to[way])

        def send_near(self, part):
            for way in (PLUS, MINUS):
                value = self.value(part, 1 if way == PLUS else 3)
                self.recv(("far", way, part), self.home.far_in.at[part, way])
                mine = slice(way * QUARTER, (way + 1) * QUARTER)
                rest = slice((1 - way) * QUARTER, (2 - way) * QUARTER)
                more = self.home.far_in[part, way].astype(jnp.float32)
                self.home.near_out[part, way, mine] = (value[mine] + more).astype(jnp.bfloat16)
                self.home.near_out[part, way, rest] = value[rest].astype(jnp.bfloat16)
                out, into = self.home.near_out.at[part, way], self.home.near_in.at[part, way]
                self.send(("near", way, part), out, into, self.ring.to[way])

        def ring_sum(self, part):
            value = self.value(part, 0)
            for way in (PLUS, MINUS):
                self.recv(("near", way, part), self.home.near_in.at[part, way])
                value = value + self.home.near_in[part, way].astype(jnp.float32)
            return value

        def send_home(self):
            self.home.home_out[...] = self.ring_sum(PAIR_A).astype(jnp.bfloat16)
            self.send(("home",), self.home.home_out, self.home.home_in, self.ring.partner)

        def finish(self, out):
            out[HALF:] = self.ring_sum(OWN_B)
            value = self.ring_sum(OWN_A)
            self.recv(("home",), self.home.home_in)
            out[:HALF] = value + self.home.home_in[...].astype(jnp.float32)

    images, texts = Sums(image, image_home, image_part), Sums(text, text_home, text_part)

    def next_sum(i, name):
        recv(("sum", name), sums_in.at[i])
        sums[i + 1] = sums[i] + sums_in[i]

    def share(i, axis, me, at, source):
        ring_sums[i, me] = sums[source]
        for d in (1, 2, 3):
            send(("sum", axis, d), sums.at[source], ring_sums.at[i, me], at[d])

    def shared(i, axis, me, into):
        for d in (1, 2, 3):
            recv(("sum", axis, d), ring_sums.at[i, step(me, 4 - d)])
        sums[into] = (ring_sums[i, 0] + ring_sums[i, 1]) + (ring_sums[i, 2] + ring_sums[i, 3])

    gather_start(image)
    gather_start(text)
    to_sibling([(OWN, 0)])
    loads[2].wait()
    for ring in (image, text):
        gather_ring(ring, 1)
        gather_pair(ring)
    for ring in (image, text):
        gather_ring(ring, 0)
    for ring in (image, text):
        arrived(ring, ("y", 1), PAIR, 0, HALF, HALF)
    to_sibling(FIRST[1:])
    gather_far(image)
    gather_far(text)
    from_sibling(FIRST)
    tiles(FIRST, 4, first_place)
    gather_pair_ring(image)
    gather_pair_ring(text)
    gather_second(image)
    to_sibling(SECOND)
    gather_second(text)
    tiles(SECOND, 4, first_place)
    gather_last(image)
    to_sibling(LAST)
    gather_last(text)
    every = FIRST + SECOND + LAST
    from_sibling(SECOND)
    tile(every, OWN, 2)
    image_parts([(OWN, 2)])
    tiles(LAST, 2, lambda i: (i, 0))
    tiles(LAST, 2, lambda i: (OWN, 1 + 2 * i))
    from_sibling(LAST)
    tile(every, PAIR, 2)
    image_parts([(PAIR, 2)])
    image_ready([(OWN, 2)])
    images.send_far(OWN_A)
    tiles(every, 2, lambda i: (PAIR, 1 + 2 * i))
    image_ready([(PAIR, 2)])
    images.send_y(2)
    images.send_far(PAIR_A)

    for i in range(3):
        sums[0, i : i + 1] = jnp.sum(totals[i], axis=0, keepdims=True)
    sums[0, 3:] = jnp.zeros((5, 128), jnp.float32)
    send(("sum", "core"), sums.at[0], sums_in.at[0], sibling)

    text_parts([(PAIR, 2), (OWN, 2)])
    texts.send_y(2)
    texts.send_far(PAIR_A)
    texts.send_far(OWN_A)
    image_parts([(PAIR, 1), (PAIR, 3)])
    next_sum(0, "core")
    send(("sum", "y"), sums.at[1], sums_in.at[1], image_partner)
    text_parts([(PAIR, 1), (PAIR, 3)])
    texts.send_y(1)
    texts.send_y(3)
    image_ready([(PAIR, 1), (PAIR, 3)])
    images.send_y(1)
    images.send_y(3)
    images.send_near(PAIR_A)
    texts.send_near(PAIR_A)
    images.send_far(OWN_B)
    texts.send_far(OWN_B)
    next_sum(1, "y")
    send(("sum", "yy"), sums.at[2], sums_in.at[2], text_partner)

    image_parts([(OWN, 1), (OWN, 3)])
    text_parts([(OWN, 1), (OWN, 3)])
    texts.send_near(OWN_A)
    image_ready([(OWN, 1), (OWN, 3)])
    images.send_near(OWN_A)
    image_parts([(PAIR, 0), (OWN, 0)])
    next_sum(2, "yy")
    share(0, "x", x, x_at, 3)
    text_parts([(PAIR, 0), (OWN, 0)])
    texts.send_y(0)
    image_ready([(PAIR, 0), (OWN, 0)])
    images.send_y(0)
    texts.send_near(OWN_B)
    images.send_near(OWN_B)
    shared(0, "x", x, 4)
    share(1, "z", z, z_at, 4)
    texts.send_home()
    images.send_home()
    shared(1, "z", z, 5)
    scalar_sums[...] = sums[5]
    images.finish(image_sum)
    texts.finish(text_sum)
    for copy in started:
        copy.wait_send()


def project_kernel(
    image_emb, text_emb, image_sum, text_sum, scalar_sums, log_scale, bias, loss, image_grad, text_grad, scale_grad, bias_grad
):
    scale = jnp.exp(jnp.full((1, 1), log_scale[0], jnp.float32))
    for emb, summed, grad in ((image_emb, image_sum, image_grad), (text_emb, text_sum, text_grad)):
        unit, norm = unit_rows(emb[...])
        value = summed[...] * scale
        grad[...] = (value - unit * jnp.sum(unit * value, axis=1, keepdims=True)) / norm
    total = jnp.sum(scalar_sums[...], axis=1, keepdims=True)
    loss[...] = total[0:1] / PAIRS
    bias_grad[...] = total[1:2]
    scale_grad[...] = scale * total[2:3]


PAIRS = 16384


def body(image_emb, text_emb, positive, log_scale, bias):
    rows, width = image_emb.shape
    images, texts = 16 * rows, 8 * rows
    low, full = jnp.bfloat16, jnp.float32
    vmem = pl.BlockSpec(memory_space=pltpu.VMEM)
    smem = pl.BlockSpec(memory_space=pltpu.SMEM)
    hbm = pl.BlockSpec(memory_space=pl.ANY)
    scalar = jax.ShapeDtypeStruct((1, 1), full)
    grad = jax.ShapeDtypeStruct((rows, width), full)
    home = [
        pltpu.VMEM((8, rows, width), full),
        pltpu.VMEM((3, 2, QUARTER, width), low), pltpu.VMEM((3, 2, QUARTER, width), low),
        pltpu.VMEM((3, 2, HALF, width), low), pltpu.VMEM((3, 2, HALF, width), low),
        pltpu.VMEM((4, HALF, width), low), pltpu.VMEM((4, HALF, width), low),
        pltpu.VMEM((HALF, width), low), pltpu.VMEM((HALF, width), low),
    ]
    log_scale, bias = log_scale.reshape(1), bias.reshape(1)
    image_sum, text_sum, scalar_sums = pl.pallas_call(
        kernel,
        out_shape=(grad, grad, jax.ShapeDtypeStruct((8, 128), full)),
        in_specs=[hbm, hbm, hbm, smem, smem],
        out_specs=(vmem,) * 3,
        scratch_shapes=[
            pltpu.VMEM((rows, width), low),
            pltpu.VMEM((rows, width), low),
            pltpu.VMEM((1, images), jnp.int32),
            pltpu.VMEM((images, width), low),
            pltpu.VMEM((texts, width), low),
            pltpu.VMEM((texts, images), low),
            pltpu.VMEM((8, rows, width), low),
            pltpu.VMEM((8, rows, width), low),
            *home,
            *home,
            pltpu.VMEM((3, 8, 128), full),
            pltpu.VMEM((6, 8, 128), full),
            pltpu.VMEM((3, 8, 128), full),
            pltpu.VMEM((2, 4, 8, 128), full),
            pltpu.SemaphoreType.DMA((len(NAMES),)),
            pltpu.SemaphoreType.DMA((len(NAMES),)),
            pltpu.SemaphoreType.DMA((3,)),
        ],
        compiler_params=pltpu.CompilerParams(collective_id=0, has_side_effects=True, vmem_limit_bytes=52 * 2**20),
    )(image_emb, text_emb, positive.reshape(1, images), log_scale, bias)
    loss, image_grad, text_grad, scale_grad, bias_grad = pl.pallas_call(
        project_kernel,
        out_shape=(scalar, grad, grad, scalar, scalar),
        in_specs=[vmem] * 5 + [smem] * 2,
        out_specs=(vmem,) * 5,
        compiler_params=pltpu.CompilerParams(vmem_limit_bytes=16 * 2**20),
    )(image_emb, text_emb, image_sum, text_sum, scalar_sums, log_scale, bias)
    return loss.reshape(()), image_grad, text_grad, scale_grad.reshape(()), bias_grad.reshape(())


def solution(mesh):
    placed = (P(("img", "txt"), None), P(("txt", "img"), None), P("img"), P(), P())
    return jax.shard_map(
        body,
        mesh=mesh,
        in_specs=placed,
        out_specs=(P(), P(("img", "txt"), None), P(("txt", "img"), None), P(), P()),
        check_vma=False,
    )
```

```python
import jax
import jax.numpy as jnp
from jax import lax
from jax.experimental import pallas as pl
from jax.experimental.pallas import tpu as pltpu
from jax.sharding import PartitionSpec as P

EPS = 1e-06
LOG2E = 1.4426950408889634
MESH = pl.DeviceIdType.MESH
OWN, PAIR = 0, 1
ROWS = 128
HALF = ROWS // 2
PLUS, MINUS = 0, 1
PART = ((0, 64), (64, 64))
SPLIT = (((0, 32), (32, 32)), ((64, 32), (96, 32)))
HOME_PART = ((0, 80), (80, 48))
HOME_SPLIT = (((0, 48), (48, 32)), ((80, 16), (96, 32)))
OWN_A, OWN_B, PAIR_A = 0, 1, 2
FIRST = [(OWN, 0), (PAIR, 0), (OWN, 1), (OWN, 3)]
SECOND = [(PAIR, 1), (PAIR, 3), (OWN, 2)]
LAST = [(PAIR, 2)]

NAMES = []
for _kind in ("image", "text"):
    NAMES += [(_kind, "y", h) for h in (0, 1)]
    NAMES += [(_kind, "y_ring", d) for d in (1, 2, 3)]
    NAMES += [(_kind, "own", way, h) for way in (PLUS, MINUS) for h in (0, 1)]
    NAMES += [(_kind, "own2", way, h) for way in (PLUS, MINUS) for h in (0, 1)]
    NAMES += [(_kind, step, way) for step in ("pair", "pair2") for way in (PLUS, MINUS)]
    NAMES += [(_kind, "y_sum", d) for d in range(4)]
    NAMES += [(_kind, step, way, part) for step in ("far", "near") for way in (PLUS, MINUS) for part in range(3)]
    NAMES += [(_kind, "home")]
NAMES += [("core", t, d) for t in (OWN, PAIR) for d in range(4)]
NAMES += [("coresum", t, d) for t in (OWN, PAIR) for d in range(4)]
NAMES += [("sum", "y", d) for d in range(1, 8)]
NAMES += [("sum", axis, d) for axis in ("x", "z") for d in (1, 2, 3)]
IDS = {name: i for i, name in enumerate(NAMES)}


def unit_rows(emb):
    values = emb.astype(jnp.float32)
    norm = jnp.sqrt(jnp.sum(values * values, axis=1, keepdims=True) + EPS)
    return values / norm, norm


PAIRS = 16384


class Ring:
    def __init__(self, kind, rows, partner, plus, minus, slot):
        self.kind, self.rows, self.partner = kind, rows, partner
        self.to = {PLUS: plus, MINUS: minus}
        self.slot = slot

    def part(self, t, d, first, count):
        return self.rows.at[pl.ds(pl.multiple_of(self.slot(t, d) * ROWS + first, 16), count)]


class Home:
    def __init__(self, own, far_out, far_in, near_out, near_in, y_out, y_in, home_out, home_in):
        self.own, self.far_out, self.far_in, self.near_out, self.near_in = own, far_out, far_in, near_out, near_in
        self.y_out, self.y_in, self.home_out, self.home_in = y_out, y_in, home_out, home_in


def kernel(
    image_emb, text_emb, positive_in, log_scale, bias,
    image_sum, text_sum, scalar_sums,
    image_in, text_in, positive, image_rows, text_rows, weight_t, core_out, core_in, *rest,
):
    image_home, text_home = Home(*rest[:9]), Home(*rest[9:18])
    totals, sums, shares, send_sem, recv_sem, load_sem = rest[18:]
    img, txt = lax.axis_index("img"), lax.axis_index("txt")
    z, yh = lax.div(img, 2), lax.rem(img, 2)
    yl, x, c = lax.div(txt, 8), lax.rem(lax.div(txt, 2), 4), lax.rem(txt, 2)

    loads = [
        pltpu.make_async_copy(src, dst, load_sem.at[i])
        for i, (src, dst) in enumerate(((image_emb, image_in), (text_emb, text_in), (positive_in, positive)))
    ]
    for load in loads:
        load.start()

    def device(z=z, yh=yh, yl=yl, x=x, c=c):
        return (z * 2 + yh, yl * 8 + x * 2 + c)

    def step(i, d):
        return lax.rem(i + d, 4)

    def other(bit, t):
        return bit + t * (1 - 2 * bit)

    sibling = device(c=1 - c)
    image_partner = device(yl=1 - yl)
    text_partner = device(yl=1 - yl, yh=1 - yh)
    x_at = {d: device(x=step(x, d)) for d in (1, 2, 3)}
    z_at = {d: device(z=step(z, d)) for d in (1, 2, 3)}

    barrier = pltpu.get_barrier_semaphore()
    y_at = {a * 4 + b * 2 + e: device(yh=other(yh, a), yl=other(yl, b), c=other(c, e)) for a in (0, 1) for b in (0, 1) for e in (0, 1)}
    del y_at[0]
    partners = [*y_at.values(), *x_at.values(), *z_at.values()]
    for partner in partners:
        pl.semaphore_signal(barrier, inc=1, device_id=partner, device_id_type=MESH)

    def image_slot(t, d, core=c):
        return other(yl, t) * 8 + step(x, d) * 2 + core

    def text_slot(t, d):
        return step(z, d) * 2 + other(yh, t)

    image = Ring("image", image_rows, image_partner, x_at[1], x_at[3], image_slot)
    text = Ring("text", text_rows, text_partner, z_at[1], z_at[3], text_slot)

    started = []

    def send(name, src, dst, to):
        i = IDS[name]
        copy = pltpu.make_async_remote_copy(
            src_ref=src, dst_ref=dst, send_sem=send_sem.at[i], recv_sem=recv_sem.at[i], device_id=to, device_id_type=MESH
        )
        copy.start()
        started.append(copy)

    def recv(name, dst):
        i = IDS[name]
        pltpu.make_async_remote_copy(
            src_ref=dst, dst_ref=dst, send_sem=send_sem.at[i], recv_sem=recv_sem.at[i], device_id=sibling, device_id_type=MESH
        ).wait_recv()

    def block(slot):
        return pl.ds(pl.multiple_of(slot * ROWS, ROWS), ROWS)

    def own_rows(load, emb, ring):
        load.wait()
        unit, _ = unit_rows(emb[...])
        ring.rows[block(ring.slot(OWN, 0)), :] = unit.astype(jnp.bfloat16)

    own_rows(loads[0], image_in, image)
    own_rows(loads[1], text_in, text)
    pl.semaphore_wait(barrier, len(partners))

    def forward(ring, name, t, d, first, count, to):
        part = ring.part(t, d, first, count)
        send((ring.kind, *name), part, part, to)

    def arrived(ring, name, t, d, first, count):
        recv((ring.kind, *name), ring.part(t, d, first, count))

    def to_sibling(blocks):
        for t, d in blocks:
            part = image_rows.at[block(image_slot(t, d))]
            send(("core", t, d), part, part, sibling)

    def from_sibling(blocks):
        for t, d in blocks:
            recv(("core", t, d), image_rows.at[block(image_slot(t, d, 1 - c))])

    def near(way):
        return 3 if way == PLUS else 1

    def gather_start(ring):
        forward(ring, ("y", 0), OWN, 0, *PART[0], ring.partner)
        for h in (1, 0):
            for way in (PLUS, MINUS):
                forward(ring, ("own", way, h), OWN, 0, *PART[h], ring.to[way])
        forward(ring, ("y", 1), OWN, 0, *PART[1], ring.partner)

    def gather_ring(ring, h):
        for way in (PLUS, MINUS):
            d = near(way)
            arrived(ring, ("own", way, h), OWN, d, *PART[h])
            forward(ring, ("own2", way, h), OWN, d, *SPLIT[h][way], ring.to[way])
            if h == 1:
                forward(ring, ("y_ring", d), OWN, d, *PART[1], ring.partner)

    def gather_pair(ring):
        arrived(ring, ("y", 0), PAIR, 0, *PART[0])
        for way in (PLUS, MINUS):
            forward(ring, ("pair", way), PAIR, 0, *PART[0], ring.to[way])

    def gather_far(ring):
        for way in (PLUS, MINUS):
            arrived(ring, ("own2", way, 1), OWN, 2, *SPLIT[1][way])
        forward(ring, ("y_ring", 2), OWN, 2, *PART[1], ring.partner)

    def gather_pair_ring(ring):
        for way in (PLUS, MINUS):
            d = near(way)
            arrived(ring, ("pair", way), PAIR, d, *PART[0])
            forward(ring, ("pair2", way), PAIR, d, *SPLIT[0][way], ring.to[way])

    def gather_second(ring):
        for d in (1, 3):
            arrived(ring, ("y_ring", d), PAIR, d, *PART[1])
        for way in (PLUS, MINUS):
            arrived(ring, ("own2", way, 0), OWN, 2, *SPLIT[0][way])

    def gather_last(ring):
        arrived(ring, ("y_ring", 2), PAIR, 2, *PART[1])
        for way in (PLUS, MINUS):
            arrived(ring, ("pair2", way), PAIR, 2, *SPLIT[0][way])

    scale = jnp.exp(jnp.full((1, 256), log_scale[0], jnp.float32))
    scale2 = scale * LOG2E
    bias2 = jnp.full((1, 256), bias[0] * LOG2E, jnp.float32)
    totals[...] = jnp.zeros_like(totals)

    def tile(blocks, t, dx):
        columns = pl.multiple_of(image_slot(t, dx, 0) * ROWS, 256)
        cosine = lax.dot_general(
            jnp.concatenate([text_rows[block(text_slot(*b)), :] for b in blocks], axis=0),
            image_rows[pl.ds(columns, 256), :], (((1,), (1,)), ((), ())), preferred_element_type=jnp.float32,
        )
        wanted = positive[:, pl.ds(columns, 256)]
        add = [jnp.zeros((8, 256), jnp.float32) for _ in range(3)]
        for n, (tt, dz) in enumerate(blocks):
            at = text_slot(tt, dz) * ROWS
            first = ((other(yl, tt) * 8 + x * 2 + c) * 8 + text_slot(tt, dz)) * ROWS
            for part in (0, HALF):
                cos = cosine[n * ROWS + part : n * ROWS + part + HALF]
                row = lax.broadcasted_iota(jnp.int32, (HALF, 256), 0)
                flip = jnp.where(row == wanted - (first + part), -1.0, 1.0)
                e = jnp.exp2((cos * scale2 + bias2) * flip)
                u = 1.0 + e
                w = (e / u) * flip
                weight_t[pl.ds(pl.multiple_of(at + part, HALF), HALF), pl.ds(columns, 256)] = w.astype(jnp.bfloat16)
                e8, u8 = e.reshape(8, 8, 256), u.reshape(8, 8, 256)
                product = e8[0]
                for k in range(1, 8):
                    product = product * u8[k] + e8[k]
                add[0] += jnp.log1p(product)
                add[1] += jnp.sum(w.reshape(8, 8, 256), axis=0)
                add[2] += jnp.sum((w * cos).reshape(8, 8, 256), axis=0)
        for i in range(3):
            totals[i] += add[i][:, :128] + add[i][:, 128:]

    def tiles(blocks, count, place):
        def body(i, carry):
            tile(blocks, *place(i))
            return carry

        lax.fori_loop(0, count, body, 0)

    def first_place(i):
        return lax.rem(i, 2) * (1 - lax.div(i, 2)), lax.div(i * (i - 1), 2)

    def place(t, d):
        return t * 4 + d

    def image_parts(blocks):
        slots = [image_slot(t, d, core) for t, d in blocks for core in (c, 1 - c)]
        lhs = jnp.concatenate([weight_t[:, block(slot)] for slot in slots], axis=1)
        out = lax.dot_general(lhs, text_rows[...], (((0,), (0,)), ((), ())), preferred_element_type=jnp.float32)
        for n, (t, d) in enumerate(blocks):
            core_out[place(t, d)] = out[n * 256 + ROWS : (n + 1) * 256].astype(jnp.bfloat16)
            send(("coresum", t, d), core_out.at[place(t, d)], core_in.at[place(t, d)], sibling)
            image_home.own[place(t, d)] = out[n * 256 : n * 256 + ROWS]

    def text_parts(blocks):
        lhs = jnp.concatenate([weight_t[block(text_slot(t, d)), :] for t, d in blocks], axis=0)
        out = jnp.dot(lhs, image_rows[...], preferred_element_type=jnp.float32)
        for n, (t, d) in enumerate(blocks):
            text_home.own[place(t, d)] = out[n * ROWS : (n + 1) * ROWS]

    def image_ready(blocks):
        for t, d in blocks:
            recv(("coresum", t, d), core_in.at[place(t, d)])

    def rows_of(h):
        return slice(HOME_PART[h][0], sum(HOME_PART[h]))

    def image_part(t, d, h):
        return image_home.own[place(t, d), rows_of(h)] + core_in[place(t, d), rows_of(h)].astype(jnp.float32)

    def text_part(t, d, h):
        return text_home.own[place(t, d), rows_of(h)]

    class Sums:
        def __init__(self, ring, home, part):
            self.ring, self.home, self.part = ring, home, part

        def send(self, name, out, into, to):
            send((self.ring.kind, *name), out, into, to)

        def recv(self, name, into):
            recv((self.ring.kind, *name), into)

        def value(self, part, d):
            if part == OWN_B:
                self.recv(("y_sum", d), self.home.y_in.at[d])
                return self.part(OWN, d, 1) + self.home.y_in[d].astype(jnp.float32)
            return self.part(OWN if part == OWN_A else PAIR, d, 0)

        def send_y(self, d):
            self.home.y_out[d] = self.part(PAIR, d, 1).astype(jnp.bfloat16)
            self.send(("y_sum", d), self.home.y_out.at[d], self.home.y_in.at[d], self.ring.partner)

        def split(self, part, way):
            h = 1 if part == OWN_B else 0
            first, count = HOME_SPLIT[h][way]
            return first - HOME_PART[h][0], count

        def send_far(self, part):
            value = self.value(part, 2).astype(jnp.bfloat16)
            for way in (PLUS, MINUS):
                first, count = self.split(part, way)
                self.home.far_out[part, way, :count] = value[first : first + count]
                out, into = self.home.far_out.at[part, way, pl.ds(0, count)], self.home.far_in.at[part, way, pl.ds(0, count)]
                self.send(("far", way, part), out, into, self.ring.to[way])

        def send_near(self, part):
            for way in (PLUS, MINUS):
                value = self.value(part, 1 if way == PLUS else 3)
                rows = value.shape[0]
                first, count = self.split(part, way)
                out, into = self.home.near_out.at[part, way, pl.ds(0, rows)], self.home.near_in.at[part, way, pl.ds(0, rows)]
                self.recv(("far", way, part), self.home.far_in.at[part, way, pl.ds(0, count)])
                more = self.home.far_in[part, way, :count].astype(jnp.float32)
                for lo, hi in ((0, first), (first, first + count), (first + count, rows)):
                    if lo < hi:
                        piece = value[lo:hi] + more if lo == first else value[lo:hi]
                        self.home.near_out[part, way, lo:hi] = piece.astype(jnp.bfloat16)
                self.send(("near", way, part), out, into, self.ring.to[way])

        def ring_sum(self, part):
            value = self.value(part, 0)
            rows = value.shape[0]
            for way in (PLUS, MINUS):
                self.recv(("near", way, part), self.home.near_in.at[part, way, pl.ds(0, rows)])
                value = value + self.home.near_in[part, way, :rows].astype(jnp.float32)
            return value

        def send_home(self):
            self.home.home_out[...] = self.ring_sum(PAIR_A).astype(jnp.bfloat16)
            self.send(("home",), self.home.home_out, self.home.home_in, self.ring.partner)

        def finish(self, out):
            out[rows_of(1)] = self.ring_sum(OWN_B)
            value = self.ring_sum(OWN_A)
            self.recv(("home",), self.home.home_in)
            out[rows_of(0)] = value + self.home.home_in[...].astype(jnp.float32)

    images, texts = Sums(image, image_home, image_part), Sums(text, text_home, text_part)

    def slot_y(d):
        return other(yh, d // 4) * 4 + other(yl, d // 2 % 2) * 2 + other(c, d % 2)

    stages = {
        "y": (0, 8, slot_y, y_at),
        "x": (1, 4, lambda d: step(x, (4 - d) % 4), x_at),
        "z": (2, 4, lambda d: step(z, (4 - d) % 4), z_at),
    }

    def share(axis):
        i, _, slot, peers = stages[axis]
        shares[i, slot(0)] = sums[i]
        for d, peer in peers.items():
            send(("sum", axis, d), sums.at[i], shares.at[i, slot(0)], peer)

    def shared(axis):
        i, count, slot, peers = stages[axis]
        for d in peers:
            recv(("sum", axis, d), shares.at[i, slot(d)])
        sums[i + 1] = sum(shares[i, k] for k in range(count))

    gather_start(image)
    gather_start(text)
    to_sibling([(OWN, 0)])
    loads[2].wait()
    for ring in (image, text):
        gather_ring(ring, 1)
        gather_pair(ring)
    for ring in (image, text):
        gather_ring(ring, 0)
    for ring in (image, text):
        arrived(ring, ("y", 1), PAIR, 0, *PART[1])
    to_sibling(FIRST[1:])
    gather_far(image)
    gather_far(text)
    from_sibling(FIRST)
    tiles(FIRST, 4, first_place)
    gather_pair_ring(image)
    gather_pair_ring(text)
    gather_second(image)
    to_sibling(SECOND)
    gather_second(text)
    tiles(SECOND, 4, first_place)
    gather_last(image)
    to_sibling(LAST)
    gather_last(text)
    every = FIRST + SECOND + LAST
    from_sibling(SECOND)
    tile(every, OWN, 2)
    from_sibling(LAST)
    tile(every, PAIR, 2)
    image_parts([(PAIR, 2), (OWN, 2)])
    tiles(every, 2, lambda i: (PAIR, 1 + 2 * i))
    image_ready([(PAIR, 2), (OWN, 2)])
    images.send_y(2)
    images.send_far(PAIR_A)
    images.send_far(OWN_A)
    tiles(LAST, 4, first_place)
    for i in range(3):
        sums[0, i : i + 1] = jnp.sum(totals[i], axis=0, keepdims=True)
    sums[0, 3:] = jnp.zeros((5, 128), jnp.float32)
    share("y")
    text_parts([(PAIR, 2), (OWN, 2)])
    texts.send_y(2)
    texts.send_far(PAIR_A)
    texts.send_far(OWN_A)
    image_parts([(PAIR, 1), (PAIR, 3)])
    shared("y")
    share("x")
    text_parts([(PAIR, 1), (PAIR, 3)])
    texts.send_y(1)
    texts.send_y(3)
    image_ready([(PAIR, 1), (PAIR, 3)])
    images.send_y(1)
    images.send_y(3)
    images.send_near(PAIR_A)
    texts.send_near(PAIR_A)
    images.send_far(OWN_B)
    image_parts([(OWN, 1), (OWN, 3)])
    shared("x")
    share("z")
    texts.send_far(OWN_B)
    image_parts([(PAIR, 0)])
    text_parts([(PAIR, 0)])
    texts.send_y(0)
    text_parts([(OWN, 1), (OWN, 3)])
    image_ready([(OWN, 1), (OWN, 3)])
    images.send_near(OWN_A)
    texts.send_near(OWN_A)
    image_ready([(PAIR, 0)])
    images.send_y(0)
    images.send_home()
    texts.send_home()
    images.send_near(OWN_B)
    texts.send_near(OWN_B)
    image_parts([(OWN, 0)])
    text_parts([(OWN, 0)])
    shared("z")
    scalar_sums[...] = sums[3]
    image_ready([(OWN, 0)])
    images.finish(image_sum)
    texts.finish(text_sum)
    for copy in started:
        copy.wait_send()


def project_kernel(
    image_emb, text_emb, image_sum, text_sum, scalar_sums, log_scale, bias, loss, image_grad, text_grad, scale_grad, bias_grad
):
    scale = jnp.exp(jnp.full((1, 1), log_scale[0], jnp.float32))
    for emb, summed, grad in ((image_emb, image_sum, image_grad), (text_emb, text_sum, text_grad)):
        unit, norm = unit_rows(emb[...])
        value = summed[...] * scale
        grad[...] = (value - unit * jnp.sum(unit * value, axis=1, keepdims=True)) / norm
    total = jnp.sum(scalar_sums[...], axis=1, keepdims=True)
    loss[...] = total[0:1] / PAIRS
    bias_grad[...] = total[1:2]
    scale_grad[...] = scale * total[2:3]


def body(image_emb, text_emb, positive, log_scale, bias):
    rows, width = image_emb.shape
    images, texts = 16 * rows, 8 * rows
    low, full = jnp.bfloat16, jnp.float32
    vmem = pl.BlockSpec(memory_space=pltpu.VMEM)
    smem = pl.BlockSpec(memory_space=pltpu.SMEM)
    hbm = pl.BlockSpec(memory_space=pl.ANY)
    scalar = jax.ShapeDtypeStruct((1, 1), full)
    grad = jax.ShapeDtypeStruct((rows, width), full)
    home = [
        pltpu.VMEM((8, rows, width), full),
        pltpu.VMEM((3, 2, 48, width), low), pltpu.VMEM((3, 2, 48, width), low),
        pltpu.VMEM((3, 2, 80, width), low), pltpu.VMEM((3, 2, 80, width), low),
        pltpu.VMEM((4, 48, width), low), pltpu.VMEM((4, 48, width), low),
        pltpu.VMEM((80, width), low), pltpu.VMEM((80, width), low),
    ]
    log_scale, bias = log_scale.reshape(1), bias.reshape(1)
    image_sum, text_sum, scalar_sums = pl.pallas_call(
        kernel,
        out_shape=(grad, grad, jax.ShapeDtypeStruct((8, 128), full)),
        in_specs=[hbm, hbm, hbm, smem, smem],
        out_specs=(vmem,) * 3,
        scratch_shapes=[
            pltpu.VMEM((rows, width), low),
            pltpu.VMEM((rows, width), low),
            pltpu.VMEM((1, images), jnp.int32),
            pltpu.VMEM((images, width), low),
            pltpu.VMEM((texts, width), low),
            pltpu.VMEM((texts, images), low),
            pltpu.VMEM((8, rows, width), low),
            pltpu.VMEM((8, rows, width), low),
            *home,
            *home,
            pltpu.VMEM((3, 8, 128), full),
            pltpu.VMEM((4, 8, 128), full),
            pltpu.VMEM((3, 8, 8, 128), full),
            pltpu.SemaphoreType.DMA((len(NAMES),)),
            pltpu.SemaphoreType.DMA((len(NAMES),)),
            pltpu.SemaphoreType.DMA((3,)),
        ],
        compiler_params=pltpu.CompilerParams(collective_id=0, has_side_effects=True, vmem_limit_bytes=52 * 2**20),
    )(*(pltpu.with_memory_space_constraint(a, pltpu.HBM) for a in (image_emb, text_emb, positive.reshape(1, images))), log_scale, bias)
    loss, image_grad, text_grad, scale_grad, bias_grad = pl.pallas_call(
        project_kernel,
        out_shape=(scalar, grad, grad, scalar, scalar),
        in_specs=[vmem] * 5 + [smem] * 2,
        out_specs=(vmem,) * 5,
        compiler_params=pltpu.CompilerParams(vmem_limit_bytes=16 * 2**20),
    )(image_emb, text_emb, image_sum, text_sum, scalar_sums, log_scale, bias)
    return loss.reshape(()), image_grad, text_grad, scale_grad.reshape(()), bias_grad.reshape(())


def solution(mesh):
    placed = (P(("img", "txt"), None), P(("txt", "img"), None), P("img"), P(), P())
    return jax.shard_map(
        body,
        mesh=mesh,
        in_specs=placed,
        out_specs=(P(), P(("img", "txt"), None), P(("txt", "img"), None), P(), P()),
        check_vma=False,
    )
```

```python
import jax
import jax.numpy as jnp
from jax import lax
from jax.experimental import pallas as pl
from jax.experimental.pallas import tpu as pltpu
from jax.sharding import PartitionSpec as P

EPS = 1e-06
LOG2E = 1.4426950408889634
MESH = pl.DeviceIdType.MESH
OWN, PAIR = 0, 1
ROWS = 128
HALF = ROWS // 2
PLUS, MINUS = 0, 1
PART = ((0, 64), (64, 64))
SPLIT = (((0, 32), (32, 32)), ((64, 32), (96, 32)))
HOME_PART = ((0, 80), (80, 48))
HOME_SPLIT = (((0, 48), (48, 32)), ((80, 16), (96, 32)))
OWN_A, OWN_B, PAIR_A = 0, 1, 2
FIRST = [(OWN, 0), (PAIR, 0), (OWN, 1), (OWN, 3)]
SECOND = [(PAIR, 1), (PAIR, 3), (OWN, 2)]
LAST = [(PAIR, 2)]

NAMES = []
for _kind in ("image", "text"):
    NAMES += [(_kind, "y", h) for h in (0, 1)]
    NAMES += [(_kind, "y_ring", d) for d in (1, 2, 3)]
    NAMES += [(_kind, "own", way, h) for way in (PLUS, MINUS) for h in (0, 1)]
    NAMES += [(_kind, "own2", way, h) for way in (PLUS, MINUS) for h in (0, 1)]
    NAMES += [(_kind, step, way) for step in ("pair", "pair2") for way in (PLUS, MINUS)]
    NAMES += [(_kind, "y_sum", d) for d in range(4)]
    NAMES += [(_kind, step, way, part) for step in ("far", "near") for way in (PLUS, MINUS) for part in range(3)]
    NAMES += [(_kind, "home")]
NAMES += [("core", t, d) for t in (OWN, PAIR) for d in range(4)]
NAMES += [("coresum", t, d) for t in (OWN, PAIR) for d in range(4)]
NAMES += [("sum", "y", d) for d in range(1, 8)]
NAMES += [("sum", axis, d) for axis in ("x", "z") for d in (1, 2, 3)]
IDS = {name: i for i, name in enumerate(NAMES)}


def unit_rows(emb):
    values = emb.astype(jnp.float32)
    norm = jnp.sqrt(jnp.sum(values * values, axis=1, keepdims=True) + EPS)
    return values / norm, norm


PAIRS = 16384


class Ring:
    def __init__(self, kind, rows, partner, plus, minus, slot):
        self.kind, self.rows, self.partner = kind, rows, partner
        self.to = {PLUS: plus, MINUS: minus}
        self.slot = slot

    def part(self, t, d, first, count):
        return self.rows.at[pl.ds(pl.multiple_of(self.slot(t, d) * ROWS + first, 16), count)]


class Home:
    def __init__(self, own, far_out, far_in, near_out, near_in, y_out, y_in, home_out, home_in):
        self.own, self.far_out, self.far_in, self.near_out, self.near_in = own, far_out, far_in, near_out, near_in
        self.y_out, self.y_in, self.home_out, self.home_in = y_out, y_in, home_out, home_in


def kernel(
    image_emb, text_emb, positive_in, log_scale, bias,
    image_sum, text_sum, scalar_sums,
    image_in, text_in, positive, image_rows, text_rows, weight_t, core_out, core_in, *rest,
):
    image_home, text_home = Home(*rest[:9]), Home(*rest[9:18])
    totals, sums, shares, send_sem, recv_sem, load_sem = rest[18:]
    img, txt = lax.axis_index("img"), lax.axis_index("txt")
    z, yh = lax.div(img, 2), lax.rem(img, 2)
    yl, x, c = lax.div(txt, 8), lax.rem(lax.div(txt, 2), 4), lax.rem(txt, 2)

    loads = [
        pltpu.make_async_copy(src, dst, load_sem.at[i])
        for i, (src, dst) in enumerate(((image_emb, image_in), (text_emb, text_in), (positive_in, positive)))
    ]
    for load in loads:
        load.start()

    def device(z=z, yh=yh, yl=yl, x=x, c=c):
        return (z * 2 + yh, yl * 8 + x * 2 + c)

    def step(i, d):
        return lax.rem(i + d, 4)

    def other(bit, t):
        return bit + t * (1 - 2 * bit)

    sibling = device(c=1 - c)
    image_partner = device(yl=1 - yl)
    text_partner = device(yl=1 - yl, yh=1 - yh)
    x_at = {d: device(x=step(x, d)) for d in (1, 2, 3)}
    z_at = {d: device(z=step(z, d)) for d in (1, 2, 3)}

    barrier = pltpu.get_barrier_semaphore()
    y_at = {a * 4 + b * 2 + e: device(yh=other(yh, a), yl=other(yl, b), c=other(c, e)) for a in (0, 1) for b in (0, 1) for e in (0, 1)}
    del y_at[0]
    partners = [*y_at.values(), *x_at.values(), *z_at.values()]
    for partner in partners:
        pl.semaphore_signal(barrier, inc=1, device_id=partner, device_id_type=MESH)

    def image_slot(t, d, core=c):
        return other(yl, t) * 8 + step(x, d) * 2 + core

    def text_slot(t, d):
        return step(z, d) * 2 + other(yh, t)

    image = Ring("image", image_rows, image_partner, x_at[1], x_at[3], image_slot)
    text = Ring("text", text_rows, text_partner, z_at[1], z_at[3], text_slot)

    started = []

    def send(name, src, dst, to):
        i = IDS[name]
        copy = pltpu.make_async_remote_copy(
            src_ref=src, dst_ref=dst, send_sem=send_sem.at[i], recv_sem=recv_sem.at[i], device_id=to, device_id_type=MESH
        )
        copy.start()
        started.append(copy)

    def recv(name, dst):
        i = IDS[name]
        pltpu.make_async_remote_copy(
            src_ref=dst, dst_ref=dst, send_sem=send_sem.at[i], recv_sem=recv_sem.at[i], device_id=sibling, device_id_type=MESH
        ).wait_recv()

    def block(slot):
        return pl.ds(pl.multiple_of(slot * ROWS, ROWS), ROWS)

    def own_rows(load, emb, ring):
        load.wait()
        unit, _ = unit_rows(emb[...])
        ring.rows[block(ring.slot(OWN, 0)), :] = unit.astype(jnp.bfloat16)

    own_rows(loads[0], image_in, image)
    own_rows(loads[1], text_in, text)
    pl.semaphore_wait(barrier, len(partners))

    def forward(ring, name, t, d, first, count, to):
        part = ring.part(t, d, first, count)
        send((ring.kind, *name), part, part, to)

    def arrived(ring, name, t, d, first, count):
        recv((ring.kind, *name), ring.part(t, d, first, count))

    def to_sibling(blocks):
        for t, d in blocks:
            part = image_rows.at[block(image_slot(t, d))]
            send(("core", t, d), part, part, sibling)

    def from_sibling(blocks):
        for t, d in blocks:
            recv(("core", t, d), image_rows.at[block(image_slot(t, d, 1 - c))])

    def near(way):
        return 3 if way == PLUS else 1

    def gather_start(ring):
        forward(ring, ("y", 0), OWN, 0, *PART[0], ring.partner)
        for h in (1, 0):
            for way in (PLUS, MINUS):
                forward(ring, ("own", way, h), OWN, 0, *PART[h], ring.to[way])
        forward(ring, ("y", 1), OWN, 0, *PART[1], ring.partner)

    def gather_ring(ring, h):
        for way in (PLUS, MINUS):
            d = near(way)
            arrived(ring, ("own", way, h), OWN, d, *PART[h])
            forward(ring, ("own2", way, h), OWN, d, *SPLIT[h][way], ring.to[way])
            if h == 1:
                forward(ring, ("y_ring", d), OWN, d, *PART[1], ring.partner)

    def gather_pair(ring):
        arrived(ring, ("y", 0), PAIR, 0, *PART[0])
        for way in (PLUS, MINUS):
            forward(ring, ("pair", way), PAIR, 0, *PART[0], ring.to[way])

    def gather_far(ring):
        for way in (PLUS, MINUS):
            arrived(ring, ("own2", way, 1), OWN, 2, *SPLIT[1][way])
        forward(ring, ("y_ring", 2), OWN, 2, *PART[1], ring.partner)

    def gather_pair_ring(ring):
        for way in (PLUS, MINUS):
            d = near(way)
            arrived(ring, ("pair", way), PAIR, d, *PART[0])
            forward(ring, ("pair2", way), PAIR, d, *SPLIT[0][way], ring.to[way])

    def gather_second(ring):
        for d in (1, 3):
            arrived(ring, ("y_ring", d), PAIR, d, *PART[1])
        for way in (PLUS, MINUS):
            arrived(ring, ("own2", way, 0), OWN, 2, *SPLIT[0][way])

    def gather_last(ring):
        arrived(ring, ("y_ring", 2), PAIR, 2, *PART[1])
        for way in (PLUS, MINUS):
            arrived(ring, ("pair2", way), PAIR, 2, *SPLIT[0][way])

    scale = jnp.exp(jnp.full((1, 256), log_scale[0], jnp.float32))
    scale2 = scale * LOG2E
    bias2 = jnp.full((1, 256), bias[0] * LOG2E, jnp.float32)
    totals[...] = jnp.zeros_like(totals)

    def tile(blocks, t, dx):
        columns = pl.multiple_of(image_slot(t, dx, 0) * ROWS, 256)
        cosine = lax.dot_general(
            jnp.concatenate([text_rows[block(text_slot(*b)), :] for b in blocks], axis=0),
            image_rows[pl.ds(columns, 256), :], (((1,), (1,)), ((), ())), preferred_element_type=jnp.float32,
        )
        wanted = positive[:, pl.ds(columns, 256)]
        add = [jnp.zeros((8, 256), jnp.float32) for _ in range(3)]
        for n, (tt, dz) in enumerate(blocks):
            at = text_slot(tt, dz) * ROWS
            first = ((other(yl, tt) * 8 + x * 2 + c) * 8 + text_slot(tt, dz)) * ROWS
            for part in (0, HALF):
                cos = cosine[n * ROWS + part : n * ROWS + part + HALF]
                row = lax.broadcasted_iota(jnp.int32, (HALF, 256), 0)
                flip = jnp.where(row == wanted - (first + part), -1.0, 1.0)
                e = jnp.exp2((cos * scale2 + bias2) * flip)
                u = 1.0 + e
                w = (e / u) * flip
                weight_t[pl.ds(pl.multiple_of(at + part, HALF), HALF), pl.ds(columns, 256)] = w.astype(jnp.bfloat16)
                e8, u8 = e.reshape(8, 8, 256), u.reshape(8, 8, 256)
                product = e8[0]
                for k in range(1, 8):
                    product = product * u8[k] + e8[k]
                add[0] += jnp.log1p(product)
                add[1] += jnp.sum(w.reshape(8, 8, 256), axis=0)
                add[2] += jnp.sum((w * cos).reshape(8, 8, 256), axis=0)
        for i in range(3):
            totals[i] += add[i][:, :128] + add[i][:, 128:]

    def tiles(blocks, count, place):
        def body(i, carry):
            tile(blocks, *place(i))
            return carry

        lax.fori_loop(0, count, body, 0)

    def first_place(i):
        return lax.rem(i, 2) * (1 - lax.div(i, 2)), lax.div(i * (i - 1), 2)

    def place(t, d):
        return t * 4 + d

    def image_parts(blocks):
        slots = [image_slot(t, d, core) for t, d in blocks for core in (c, 1 - c)]
        lhs = jnp.concatenate([weight_t[:, block(slot)] for slot in slots], axis=1)
        out = lax.dot_general(lhs, text_rows[...], (((0,), (0,)), ((), ())), preferred_element_type=jnp.float32)
        for n, (t, d) in enumerate(blocks):
            core_out[place(t, d)] = out[n * 256 + ROWS : (n + 1) * 256].astype(jnp.bfloat16)
            send(("coresum", t, d), core_out.at[place(t, d)], core_in.at[place(t, d)], sibling)
            image_home.own[place(t, d)] = out[n * 256 : n * 256 + ROWS]

    def text_parts(blocks):
        lhs = jnp.concatenate([weight_t[block(text_slot(t, d)), :] for t, d in blocks], axis=0)
        out = jnp.dot(lhs, image_rows[...], preferred_element_type=jnp.float32)
        for n, (t, d) in enumerate(blocks):
            text_home.own[place(t, d)] = out[n * ROWS : (n + 1) * ROWS]

    def image_ready(blocks):
        for t, d in blocks:
            recv(("coresum", t, d), core_in.at[place(t, d)])

    def rows_of(h):
        return slice(HOME_PART[h][0], sum(HOME_PART[h]))

    def image_part(t, d, h):
        return image_home.own[place(t, d), rows_of(h)] + core_in[place(t, d), rows_of(h)].astype(jnp.float32)

    def text_part(t, d, h):
        return text_home.own[place(t, d), rows_of(h)]

    class Sums:
        def __init__(self, ring, home, part):
            self.ring, self.home, self.part = ring, home, part

        def send(self, name, out, into, to):
            send((self.ring.kind, *name), out, into, to)

        def recv(self, name, into):
            recv((self.ring.kind, *name), into)

        def value(self, part, d):
            if part == OWN_B:
                self.recv(("y_sum", d), self.home.y_in.at[d])
                return self.part(OWN, d, 1) + self.home.y_in[d].astype(jnp.float32)
            return self.part(OWN if part == OWN_A else PAIR, d, 0)

        def send_y(self, d):
            self.home.y_out[d] = self.part(PAIR, d, 1).astype(jnp.bfloat16)
            self.send(("y_sum", d), self.home.y_out.at[d], self.home.y_in.at[d], self.ring.partner)

        def split(self, part, way):
            h = 1 if part == OWN_B else 0
            first, count = HOME_SPLIT[h][way]
            return first - HOME_PART[h][0], count

        def send_far(self, part):
            value = self.value(part, 2).astype(jnp.bfloat16)
            for way in (PLUS, MINUS):
                first, count = self.split(part, way)
                self.home.far_out[part, way, :count] = value[first : first + count]
                out, into = self.home.far_out.at[part, way, pl.ds(0, count)], self.home.far_in.at[part, way, pl.ds(0, count)]
                self.send(("far", way, part), out, into, self.ring.to[way])

        def send_near(self, part):
            for way in (PLUS, MINUS):
                value = self.value(part, 1 if way == PLUS else 3)
                rows = value.shape[0]
                first, count = self.split(part, way)
                out, into = self.home.near_out.at[part, way, pl.ds(0, rows)], self.home.near_in.at[part, way, pl.ds(0, rows)]
                self.recv(("far", way, part), self.home.far_in.at[part, way, pl.ds(0, count)])
                more = self.home.far_in[part, way, :count].astype(jnp.float32)
                for lo, hi in ((0, first), (first, first + count), (first + count, rows)):
                    if lo < hi:
                        piece = value[lo:hi] + more if lo == first else value[lo:hi]
                        self.home.near_out[part, way, lo:hi] = piece.astype(jnp.bfloat16)
                self.send(("near", way, part), out, into, self.ring.to[way])

        def ring_sum(self, part):
            value = self.value(part, 0)
            rows = value.shape[0]
            for way in (PLUS, MINUS):
                self.recv(("near", way, part), self.home.near_in.at[part, way, pl.ds(0, rows)])
                value = value + self.home.near_in[part, way, :rows].astype(jnp.float32)
            return value

        def send_home(self):
            self.home.home_out[...] = self.ring_sum(PAIR_A).astype(jnp.bfloat16)
            self.send(("home",), self.home.home_out, self.home.home_in, self.ring.partner)

        def finish(self, out):
            out[rows_of(1)] = self.ring_sum(OWN_B)
            value = self.ring_sum(OWN_A)
            self.recv(("home",), self.home.home_in)
            out[rows_of(0)] = value + self.home.home_in[...].astype(jnp.float32)

    images, texts = Sums(image, image_home, image_part), Sums(text, text_home, text_part)

    def slot_y(d):
        return other(yh, d // 4) * 4 + other(yl, d // 2 % 2) * 2 + other(c, d % 2)

    stages = {
        "y": (0, 8, slot_y, y_at),
        "x": (1, 4, lambda d: step(x, (4 - d) % 4), x_at),
        "z": (2, 4, lambda d: step(z, (4 - d) % 4), z_at),
    }

    def share(axis):
        i, _, slot, peers = stages[axis]
        shares[i, slot(0)] = sums[i]
        for d, peer in peers.items():
            send(("sum", axis, d), sums.at[i], shares.at[i, slot(0)], peer)

    def shared(axis):
        i, count, slot, peers = stages[axis]
        for d in peers:
            recv(("sum", axis, d), shares.at[i, slot(d)])
        sums[i + 1] = sum(shares[i, k] for k in range(count))

    gather_start(image)
    gather_start(text)
    to_sibling([(OWN, 0)])
    loads[2].wait()
    for ring in (image, text):
        gather_ring(ring, 1)
        gather_pair(ring)
    for ring in (image, text):
        gather_ring(ring, 0)
    for ring in (image, text):
        arrived(ring, ("y", 1), PAIR, 0, *PART[1])
    to_sibling(FIRST[1:])
    gather_far(image)
    gather_far(text)
    from_sibling(FIRST)
    tiles(FIRST, 2, lambda i: (i, 0))
    gather_pair_ring(text)
    gather_pair_ring(image)
    tiles(FIRST, 2, lambda i: (OWN, 1 + 2 * i))
    gather_second(image)
    to_sibling(SECOND)
    gather_second(text)
    tiles(SECOND, 4, first_place)
    gather_last(image)
    to_sibling(LAST)
    gather_last(text)
    every = FIRST + SECOND + LAST
    gathered = len(started)
    from_sibling(SECOND)
    tile(every, OWN, 2)
    from_sibling(LAST)
    tile(every, PAIR, 2)
    image_parts([(PAIR, 2), (OWN, 2)])
    tiles(every, 2, lambda i: (PAIR, 1 + 2 * i))
    image_ready([(PAIR, 2), (OWN, 2)])
    images.send_y(2)
    images.send_far(PAIR_A)
    images.send_far(OWN_A)
    tiles(LAST, 4, first_place)
    for i in range(3):
        sums[0, i : i + 1] = jnp.sum(totals[i], axis=0, keepdims=True)
    sums[0, 3:] = jnp.zeros((5, 128), jnp.float32)
    share("y")
    text_parts([(PAIR, 2), (OWN, 2)])
    texts.send_y(2)
    texts.send_far(PAIR_A)
    texts.send_far(OWN_A)
    image_parts([(PAIR, 1), (PAIR, 3)])
    shared("y")
    share("x")
    text_parts([(PAIR, 1), (PAIR, 3)])
    texts.send_y(1)
    texts.send_y(3)
    image_ready([(PAIR, 1), (PAIR, 3)])
    images.send_y(1)
    images.send_y(3)
    images.send_near(PAIR_A)
    texts.send_near(PAIR_A)
    images.send_far(OWN_B)
    image_parts([(OWN, 1), (OWN, 3)])
    shared("x")
    share("z")
    texts.send_far(OWN_B)
    image_parts([(PAIR, 0)])
    text_parts([(PAIR, 0)])
    texts.send_y(0)
    text_parts([(OWN, 1), (OWN, 3)])
    image_ready([(OWN, 1), (OWN, 3)])
    images.send_near(OWN_A)
    texts.send_near(OWN_A)
    image_ready([(PAIR, 0)])
    images.send_y(0)
    images.send_home()
    texts.send_home()
    images.send_near(OWN_B)
    texts.send_near(OWN_B)
    for copy in started[:gathered]:
        copy.wait_send()
    image_parts([(OWN, 0)])
    text_parts([(OWN, 0)])
    for copy in started[gathered:]:
        copy.wait_send()
    shared("z")
    scalar_sums[...] = sums[3]
    image_ready([(OWN, 0)])
    images.finish(image_sum)
    texts.finish(text_sum)


def project_kernel(
    image_emb, text_emb, image_sum, text_sum, scalar_sums, log_scale, bias, loss, image_grad, text_grad, scale_grad, bias_grad
):
    scale = jnp.exp(jnp.full((1, 1), log_scale[0], jnp.float32))
    for emb, summed, grad in ((image_emb, image_sum, image_grad), (text_emb, text_sum, text_grad)):
        unit, norm = unit_rows(emb[...])
        value = summed[...] * scale
        grad[...] = (value - unit * jnp.sum(unit * value, axis=1, keepdims=True)) / norm
    total = jnp.sum(scalar_sums[...], axis=1, keepdims=True)
    loss[...] = total[0:1] / PAIRS
    bias_grad[...] = total[1:2]
    scale_grad[...] = scale * total[2:3]


def body(image_emb, text_emb, positive, log_scale, bias):
    rows, width = image_emb.shape
    images, texts = 16 * rows, 8 * rows
    low, full = jnp.bfloat16, jnp.float32
    vmem = pl.BlockSpec(memory_space=pltpu.VMEM)
    smem = pl.BlockSpec(memory_space=pltpu.SMEM)
    hbm = pl.BlockSpec(memory_space=pl.ANY)
    scalar = jax.ShapeDtypeStruct((1, 1), full)
    grad = jax.ShapeDtypeStruct((rows, width), full)
    home = [
        pltpu.VMEM((8, rows, width), full),
        pltpu.VMEM((3, 2, 48, width), low), pltpu.VMEM((3, 2, 48, width), low),
        pltpu.VMEM((3, 2, 80, width), low), pltpu.VMEM((3, 2, 80, width), low),
        pltpu.VMEM((4, 48, width), low), pltpu.VMEM((4, 48, width), low),
        pltpu.VMEM((80, width), low), pltpu.VMEM((80, width), low),
    ]
    log_scale, bias = log_scale.reshape(1), bias.reshape(1)
    image_sum, text_sum, scalar_sums = pl.pallas_call(
        kernel,
        out_shape=(grad, grad, jax.ShapeDtypeStruct((8, 128), full)),
        in_specs=[hbm, hbm, hbm, smem, smem],
        out_specs=(vmem,) * 3,
        scratch_shapes=[
            pltpu.VMEM((rows, width), low),
            pltpu.VMEM((rows, width), low),
            pltpu.VMEM((1, images), jnp.int32),
            pltpu.VMEM((images, width), low),
            pltpu.VMEM((texts, width), low),
            pltpu.VMEM((texts, images), low),
            pltpu.VMEM((8, rows, width), low),
            pltpu.VMEM((8, rows, width), low),
            *home,
            *home,
            pltpu.VMEM((3, 8, 128), full),
            pltpu.VMEM((4, 8, 128), full),
            pltpu.VMEM((3, 8, 8, 128), full),
            pltpu.SemaphoreType.DMA((len(NAMES),)),
            pltpu.SemaphoreType.DMA((len(NAMES),)),
            pltpu.SemaphoreType.DMA((3,)),
        ],
        compiler_params=pltpu.CompilerParams(collective_id=0, has_side_effects=True, vmem_limit_bytes=52 * 2**20),
    )(*(pltpu.with_memory_space_constraint(a, pltpu.HBM) for a in (image_emb, text_emb, positive.reshape(1, images))), log_scale, bias)
    loss, image_grad, text_grad, scale_grad, bias_grad = pl.pallas_call(
        project_kernel,
        out_shape=(scalar, grad, grad, scalar, scalar),
        in_specs=[vmem] * 5 + [smem] * 2,
        out_specs=(vmem,) * 5,
        compiler_params=pltpu.CompilerParams(vmem_limit_bytes=16 * 2**20),
    )(image_emb, text_emb, image_sum, text_sum, scalar_sums, log_scale, bias)
    return loss.reshape(()), image_grad, text_grad, scale_grad.reshape(()), bias_grad.reshape(())


def solution(mesh):
    placed = (P(("img", "txt"), None), P(("txt", "img"), None), P("img"), P(), P())
    return jax.shard_map(
        body,
        mesh=mesh,
        in_specs=placed,
        out_specs=(P(), P(("img", "txt"), None), P(("txt", "img"), None), P(), P()),
        check_vma=False,
    )
```

```python
import jax
import jax.numpy as jnp
from jax import lax
from jax.experimental import pallas as pl
from jax.experimental.pallas import tpu as pltpu
from jax.sharding import PartitionSpec as P

EPS = 1e-06
LOG2E = 1.4426950408889634
MESH = pl.DeviceIdType.MESH
OWN, PAIR = 0, 1
ROWS = 128
HALF = ROWS // 2
PLUS, MINUS = 0, 1
PART = ((0, 64), (64, 64))
SPLIT = (((0, 32), (32, 32)), ((64, 32), (96, 32)))
HOME_PART = ((0, 80), (80, 48))
HOME_SPLIT = (((0, 48), (48, 32)), ((80, 16), (96, 32)))
OWN_A, OWN_B, PAIR_A = 0, 1, 2
FIRST = [(OWN, 0), (PAIR, 0), (OWN, 1), (OWN, 3)]
SECOND = [(PAIR, 1), (PAIR, 3), (OWN, 2)]
LAST = [(PAIR, 2)]

NAMES = []
for _kind in ("image", "text"):
    NAMES += [(_kind, "y", h) for h in (0, 1)]
    NAMES += [(_kind, "y_ring", d) for d in (1, 2, 3)]
    NAMES += [(_kind, "own", way, h) for way in (PLUS, MINUS) for h in (0, 1)]
    NAMES += [(_kind, "own2", way, h) for way in (PLUS, MINUS) for h in (0, 1)]
    NAMES += [(_kind, step, way) for step in ("pair", "pair2") for way in (PLUS, MINUS)]
    NAMES += [(_kind, "y_sum", d) for d in range(4)]
    NAMES += [(_kind, step, way, part) for step in ("far", "near") for way in (PLUS, MINUS) for part in range(3)]
    NAMES += [(_kind, "home")]
NAMES += [("core", t, d) for t in (OWN, PAIR) for d in range(4)]
NAMES += [("coresum", t, d) for t in (OWN, PAIR) for d in range(4)]
NAMES += [("sum", "y", d) for d in range(1, 8)]
NAMES += [("sum", axis, d) for axis in ("x", "z") for d in (1, 2, 3)]
IDS = {name: i for i, name in enumerate(NAMES)}


def unit_rows(emb):
    values = emb.astype(jnp.float32)
    norm = jnp.sqrt(jnp.sum(values * values, axis=1, keepdims=True) + EPS)
    return values / norm, norm


PAIRS = 16384


class Ring:
    def __init__(self, kind, rows, partner, plus, minus, slot):
        self.kind, self.rows, self.partner = kind, rows, partner
        self.to = {PLUS: plus, MINUS: minus}
        self.slot = slot

    def part(self, t, d, first, count):
        return self.rows.at[pl.ds(pl.multiple_of(self.slot(t, d) * ROWS + first, 16), count)]


class Home:
    def __init__(self, own, far_out, far_in, near_out, near_in, y_out, y_in, home_out, home_in):
        self.own, self.far_out, self.far_in, self.near_out, self.near_in = own, far_out, far_in, near_out, near_in
        self.y_out, self.y_in, self.home_out, self.home_in = y_out, y_in, home_out, home_in


def kernel(
    image_emb, text_emb, positive_in, log_scale, bias,
    image_sum, text_sum, scalar_sums,
    image_in, text_in, positive, image_rows, text_rows, weight_t, core_out, core_in, *rest,
):
    image_home, text_home = Home(*rest[:9]), Home(*rest[9:18])
    totals, sums, shares, send_sem, recv_sem, load_sem = rest[18:]
    img, txt = lax.axis_index("img"), lax.axis_index("txt")
    z, yh = lax.div(img, 2), lax.rem(img, 2)
    yl, x, c = lax.div(txt, 8), lax.rem(lax.div(txt, 2), 4), lax.rem(txt, 2)

    loads = [
        pltpu.make_async_copy(src, dst, load_sem.at[i])
        for i, (src, dst) in enumerate(((image_emb, image_in), (text_emb, text_in), (positive_in, positive)))
    ]
    for load in loads:
        load.start()

    def device(z=z, yh=yh, yl=yl, x=x, c=c):
        return (z * 2 + yh, yl * 8 + x * 2 + c)

    def step(i, d):
        return lax.rem(i + d, 4)

    def other(bit, t):
        return bit + t * (1 - 2 * bit)

    sibling = device(c=1 - c)
    image_partner = device(yl=1 - yl)
    text_partner = device(yl=1 - yl, yh=1 - yh)
    x_at = {d: device(x=step(x, d)) for d in (1, 2, 3)}
    z_at = {d: device(z=step(z, d)) for d in (1, 2, 3)}

    barrier = pltpu.get_barrier_semaphore()
    y_at = {a * 4 + b * 2 + e: device(yh=other(yh, a), yl=other(yl, b), c=other(c, e)) for a in (0, 1) for b in (0, 1) for e in (0, 1)}
    del y_at[0]
    partners = [*y_at.values(), *x_at.values(), *z_at.values()]
    for partner in partners:
        pl.semaphore_signal(barrier, inc=1, device_id=partner, device_id_type=MESH)

    def image_slot(t, d, core=c):
        return other(yl, t) * 8 + step(x, d) * 2 + core

    def text_slot(t, d):
        return step(z, d) * 2 + other(yh, t)

    image = Ring("image", image_rows, image_partner, x_at[1], x_at[3], image_slot)
    text = Ring("text", text_rows, text_partner, z_at[1], z_at[3], text_slot)

    started = []

    def send(name, src, dst, to):
        i = IDS[name]
        copy = pltpu.make_async_remote_copy(
            src_ref=src, dst_ref=dst, send_sem=send_sem.at[i], recv_sem=recv_sem.at[i], device_id=to, device_id_type=MESH
        )
        copy.start()
        started.append(copy)

    def recv(name, dst):
        i = IDS[name]
        pltpu.make_async_remote_copy(
            src_ref=dst, dst_ref=dst, send_sem=send_sem.at[i], recv_sem=recv_sem.at[i], device_id=sibling, device_id_type=MESH
        ).wait_recv()

    def block(slot):
        return pl.ds(pl.multiple_of(slot * ROWS, ROWS), ROWS)

    def own_rows(load, emb, ring):
        load.wait()
        unit, _ = unit_rows(emb[...])
        ring.rows[block(ring.slot(OWN, 0)), :] = unit.astype(jnp.bfloat16)

    own_rows(loads[0], image_in, image)
    own_rows(loads[1], text_in, text)
    pl.semaphore_wait(barrier, len(partners))

    def forward(ring, name, t, d, first, count, to):
        part = ring.part(t, d, first, count)
        send((ring.kind, *name), part, part, to)

    def arrived(ring, name, t, d, first, count):
        recv((ring.kind, *name), ring.part(t, d, first, count))

    def to_sibling(blocks):
        for t, d in blocks:
            part = image_rows.at[block(image_slot(t, d))]
            send(("core", t, d), part, part, sibling)

    def from_sibling(blocks):
        for t, d in blocks:
            recv(("core", t, d), image_rows.at[block(image_slot(t, d, 1 - c))])

    def near(way):
        return 3 if way == PLUS else 1

    def gather_start(ring):
        forward(ring, ("y", 0), OWN, 0, *PART[0], ring.partner)
        for h in (1, 0):
            for way in (PLUS, MINUS):
                forward(ring, ("own", way, h), OWN, 0, *PART[h], ring.to[way])
        forward(ring, ("y", 1), OWN, 0, *PART[1], ring.partner)

    def gather_ring(ring, h):
        for way in (PLUS, MINUS):
            d = near(way)
            arrived(ring, ("own", way, h), OWN, d, *PART[h])
            forward(ring, ("own2", way, h), OWN, d, *SPLIT[h][way], ring.to[way])
            if h == 1:
                forward(ring, ("y_ring", d), OWN, d, *PART[1], ring.partner)

    def gather_pair(ring):
        arrived(ring, ("y", 0), PAIR, 0, *PART[0])
        for way in (PLUS, MINUS):
            forward(ring, ("pair", way), PAIR, 0, *PART[0], ring.to[way])

    def gather_far(ring):
        for way in (PLUS, MINUS):
            arrived(ring, ("own2", way, 1), OWN, 2, *SPLIT[1][way])
        forward(ring, ("y_ring", 2), OWN, 2, *PART[1], ring.partner)

    def gather_pair_ring(ring):
        for way in (PLUS, MINUS):
            d = near(way)
            arrived(ring, ("pair", way), PAIR, d, *PART[0])
            forward(ring, ("pair2", way), PAIR, d, *SPLIT[0][way], ring.to[way])

    def gather_second(ring):
        for d in (1, 3):
            arrived(ring, ("y_ring", d), PAIR, d, *PART[1])
        for way in (PLUS, MINUS):
            arrived(ring, ("own2", way, 0), OWN, 2, *SPLIT[0][way])

    def gather_last(ring):
        arrived(ring, ("y_ring", 2), PAIR, 2, *PART[1])
        for way in (PLUS, MINUS):
            arrived(ring, ("pair2", way), PAIR, 2, *SPLIT[0][way])

    scale = jnp.exp(jnp.full((1, 256), log_scale[0], jnp.float32))
    scale2 = scale * LOG2E
    bias2 = jnp.full((1, 256), bias[0] * LOG2E, jnp.float32)
    totals[...] = jnp.zeros_like(totals)

    def tile(blocks, t, dx):
        columns = pl.multiple_of(image_slot(t, dx, 0) * ROWS, 256)
        cosine = lax.dot_general(
            jnp.concatenate([text_rows[block(text_slot(*b)), :] for b in blocks], axis=0),
            image_rows[pl.ds(columns, 256), :], (((1,), (1,)), ((), ())), preferred_element_type=jnp.float32,
        )
        wanted = positive[:, pl.ds(columns, 256)]
        add = [jnp.zeros((8, 256), jnp.float32) for _ in range(3)]
        for n, (tt, dz) in enumerate(blocks):
            at = text_slot(tt, dz) * ROWS
            first = ((other(yl, tt) * 8 + x * 2 + c) * 8 + text_slot(tt, dz)) * ROWS
            for part in (0, HALF):
                cos = cosine[n * ROWS + part : n * ROWS + part + HALF]
                row = lax.broadcasted_iota(jnp.int32, (HALF, 256), 0)
                flip = jnp.where(row == wanted - (first + part), -1.0, 1.0)
                e = jnp.exp2((cos * scale2 + bias2) * flip)
                u = 1.0 + e
                w = (e / u) * flip
                weight_t[pl.ds(pl.multiple_of(at + part, HALF), HALF), pl.ds(columns, 256)] = w.astype(jnp.bfloat16)
                e8, u8 = e.reshape(8, 8, 256), u.reshape(8, 8, 256)
                product = e8[0]
                for k in range(1, 8):
                    product = product * u8[k] + e8[k]
                add[0] += jnp.log(1.0 + product)
                add[1] += jnp.sum(w.reshape(8, 8, 256), axis=0)
                add[2] += jnp.sum((w * cos).reshape(8, 8, 256), axis=0)
        for i in range(3):
            totals[i] += add[i][:, :128] + add[i][:, 128:]

    def tiles(blocks, count, place):
        def body(i, carry):
            tile(blocks, *place(i))
            return carry

        lax.fori_loop(0, count, body, 0)

    def first_place(i):
        return lax.rem(i, 2) * (1 - lax.div(i, 2)), lax.div(i * (i - 1), 2)

    def place(t, d):
        return t * 4 + d

    def image_parts(blocks):
        slots = [image_slot(t, d, core) for t, d in blocks for core in (c, 1 - c)]
        lhs = jnp.concatenate([weight_t[:, block(slot)] for slot in slots], axis=1)
        out = lax.dot_general(lhs, text_rows[...], (((0,), (0,)), ((), ())), preferred_element_type=jnp.float32)
        for n, (t, d) in enumerate(blocks):
            core_out[place(t, d)] = out[n * 256 + ROWS : (n + 1) * 256].astype(jnp.bfloat16)
            send(("coresum", t, d), core_out.at[place(t, d)], core_in.at[place(t, d)], sibling)
            image_home.own[place(t, d)] = out[n * 256 : n * 256 + ROWS]

    def text_parts(blocks):
        lhs = jnp.concatenate([weight_t[block(text_slot(t, d)), :] for t, d in blocks], axis=0)
        out = jnp.dot(lhs, image_rows[...], preferred_element_type=jnp.float32)
        for n, (t, d) in enumerate(blocks):
            text_home.own[place(t, d)] = out[n * ROWS : (n + 1) * ROWS]

    def image_ready(blocks):
        for t, d in blocks:
            recv(("coresum", t, d), core_in.at[place(t, d)])

    def rows_of(h):
        return slice(HOME_PART[h][0], sum(HOME_PART[h]))

    def image_part(t, d, h):
        return image_home.own[place(t, d), rows_of(h)] + core_in[place(t, d), rows_of(h)].astype(jnp.float32)

    def text_part(t, d, h):
        return text_home.own[place(t, d), rows_of(h)]

    class Sums:
        def __init__(self, ring, home, part):
            self.ring, self.home, self.part = ring, home, part

        def send(self, name, out, into, to):
            send((self.ring.kind, *name), out, into, to)

        def recv(self, name, into):
            recv((self.ring.kind, *name), into)

        def value(self, part, d):
            if part == OWN_B:
                self.recv(("y_sum", d), self.home.y_in.at[d])
                return self.part(OWN, d, 1) + self.home.y_in[d].astype(jnp.float32)
            return self.part(OWN if part == OWN_A else PAIR, d, 0)

        def send_y(self, d):
            self.home.y_out[d] = self.part(PAIR, d, 1).astype(jnp.bfloat16)
            self.send(("y_sum", d), self.home.y_out.at[d], self.home.y_in.at[d], self.ring.partner)

        def split(self, part, way):
            h = 1 if part == OWN_B else 0
            first, count = HOME_SPLIT[h][way]
            return first - HOME_PART[h][0], count

        def send_far(self, part):
            value = self.value(part, 2).astype(jnp.bfloat16)
            for way in (PLUS, MINUS):
                first, count = self.split(part, way)
                self.home.far_out[part, way, :count] = value[first : first + count]
                out, into = self.home.far_out.at[part, way, pl.ds(0, count)], self.home.far_in.at[part, way, pl.ds(0, count)]
                self.send(("far", way, part), out, into, self.ring.to[way])

        def send_near(self, part):
            for way in (PLUS, MINUS):
                value = self.value(part, 1 if way == PLUS else 3)
                rows = value.shape[0]
                first, count = self.split(part, way)
                out, into = self.home.near_out.at[part, way, pl.ds(0, rows)], self.home.near_in.at[part, way, pl.ds(0, rows)]
                self.recv(("far", way, part), self.home.far_in.at[part, way, pl.ds(0, count)])
                more = self.home.far_in[part, way, :count].astype(jnp.float32)
                for lo, hi in ((0, first), (first, first + count), (first + count, rows)):
                    if lo < hi:
                        piece = value[lo:hi] + more if lo == first else value[lo:hi]
                        self.home.near_out[part, way, lo:hi] = piece.astype(jnp.bfloat16)
                self.send(("near", way, part), out, into, self.ring.to[way])

        def ring_sum(self, part):
            value = self.value(part, 0)
            rows = value.shape[0]
            for way in (PLUS, MINUS):
                self.recv(("near", way, part), self.home.near_in.at[part, way, pl.ds(0, rows)])
                value = value + self.home.near_in[part, way, :rows].astype(jnp.float32)
            return value

        def send_home(self):
            self.home.home_out[...] = self.ring_sum(PAIR_A).astype(jnp.bfloat16)
            self.send(("home",), self.home.home_out, self.home.home_in, self.ring.partner)

        def finish(self, out):
            out[rows_of(1)] = self.ring_sum(OWN_B)
            value = self.ring_sum(OWN_A)
            self.recv(("home",), self.home.home_in)
            out[rows_of(0)] = value + self.home.home_in[...].astype(jnp.float32)

    images, texts = Sums(image, image_home, image_part), Sums(text, text_home, text_part)

    def slot_y(d):
        return other(yh, d // 4) * 4 + other(yl, d // 2 % 2) * 2 + other(c, d % 2)

    stages = {
        "y": (0, 8, slot_y, y_at),
        "x": (1, 4, lambda d: step(x, (4 - d) % 4), x_at),
        "z": (2, 4, lambda d: step(z, (4 - d) % 4), z_at),
    }

    def share(axis):
        i, _, slot, peers = stages[axis]
        shares[i, slot(0)] = sums[i]
        for d, peer in peers.items():
            send(("sum", axis, d), sums.at[i], shares.at[i, slot(0)], peer)

    def shared(axis):
        i, count, slot, peers = stages[axis]
        for d in peers:
            recv(("sum", axis, d), shares.at[i, slot(d)])
        sums[i + 1] = sum(shares[i, k] for k in range(count))

    gather_start(image)
    gather_start(text)
    to_sibling([(OWN, 0)])
    loads[2].wait()
    for ring in (image, text):
        gather_ring(ring, 1)
        gather_pair(ring)
    for ring in (image, text):
        gather_ring(ring, 0)
    for ring in (image, text):
        arrived(ring, ("y", 1), PAIR, 0, *PART[1])
    to_sibling(FIRST[1:])
    gather_far(image)
    gather_far(text)
    from_sibling(FIRST[:2])
    tiles(FIRST, 2, lambda i: (i, 0))
    gather_pair_ring(text)
    gather_pair_ring(image)
    from_sibling(FIRST[2:])
    tiles(FIRST, 2, lambda i: (OWN, 1 + 2 * i))
    gather_second(image)
    to_sibling(SECOND)
    gather_second(text)
    tiles(SECOND, 4, first_place)
    gather_last(image)
    to_sibling(LAST)
    gather_last(text)
    every = FIRST + SECOND + LAST
    gathered = len(started)
    from_sibling(SECOND)
    tile(every, OWN, 2)
    from_sibling(LAST)
    tile(every, PAIR, 2)
    image_parts([(PAIR, 2), (OWN, 2)])
    tiles(every, 2, lambda i: (PAIR, 1 + 2 * i))
    image_ready([(PAIR, 2), (OWN, 2)])
    images.send_y(2)
    images.send_far(PAIR_A)
    images.send_far(OWN_A)
    tiles(LAST, 4, first_place)
    for i in range(3):
        sums[0, i : i + 1] = jnp.sum(totals[i], axis=0, keepdims=True)
    sums[0, 3:] = jnp.zeros((5, 128), jnp.float32)
    share("y")
    text_parts([(PAIR, 2), (OWN, 2)])
    texts.send_y(2)
    texts.send_far(PAIR_A)
    texts.send_far(OWN_A)
    image_parts([(PAIR, 1), (PAIR, 3)])
    shared("y")
    share("x")
    text_parts([(PAIR, 1), (PAIR, 3)])
    texts.send_y(1)
    texts.send_y(3)
    image_ready([(PAIR, 1), (PAIR, 3)])
    images.send_y(1)
    images.send_y(3)
    images.send_near(PAIR_A)
    texts.send_near(PAIR_A)
    images.send_far(OWN_B)
    image_parts([(OWN, 1), (OWN, 3)])
    shared("x")
    share("z")
    texts.send_far(OWN_B)
    image_parts([(PAIR, 0)])
    text_parts([(PAIR, 0)])
    texts.send_y(0)
    text_parts([(OWN, 1), (OWN, 3)])
    image_ready([(OWN, 1), (OWN, 3)])
    images.send_near(OWN_A)
    texts.send_near(OWN_A)
    image_ready([(PAIR, 0)])
    images.send_y(0)
    images.send_home()
    texts.send_home()
    images.send_near(OWN_B)
    texts.send_near(OWN_B)
    for copy in started[:gathered]:
        copy.wait_send()
    image_parts([(OWN, 0)])
    text_parts([(OWN, 0)])
    for copy in started[gathered:]:
        copy.wait_send()
    shared("z")
    scalar_sums[...] = sums[3]
    image_ready([(OWN, 0)])
    images.finish(image_sum)
    texts.finish(text_sum)


def project_kernel(
    image_emb, text_emb, image_sum, text_sum, scalar_sums, log_scale, bias, loss, image_grad, text_grad, scale_grad, bias_grad
):
    scale = jnp.exp(jnp.full((1, 1), log_scale[0], jnp.float32))
    for emb, summed, grad in ((image_emb, image_sum, image_grad), (text_emb, text_sum, text_grad)):
        unit, norm = unit_rows(emb[...])
        value = summed[...] * scale
        grad[...] = (value - unit * jnp.sum(unit * value, axis=1, keepdims=True)) / norm
    total = jnp.sum(scalar_sums[...], axis=1, keepdims=True)
    loss[...] = total[0:1] / PAIRS
    bias_grad[...] = total[1:2]
    scale_grad[...] = scale * total[2:3]


def body(image_emb, text_emb, positive, log_scale, bias):
    rows, width = image_emb.shape
    images, texts = 16 * rows, 8 * rows
    low, full = jnp.bfloat16, jnp.float32
    vmem = pl.BlockSpec(memory_space=pltpu.VMEM)
    smem = pl.BlockSpec(memory_space=pltpu.SMEM)
    hbm = pl.BlockSpec(memory_space=pl.ANY)
    scalar = jax.ShapeDtypeStruct((1, 1), full)
    grad = jax.ShapeDtypeStruct((rows, width), full)
    home = [
        pltpu.VMEM((8, rows, width), full),
        pltpu.VMEM((3, 2, 48, width), low), pltpu.VMEM((3, 2, 48, width), low),
        pltpu.VMEM((3, 2, 80, width), low), pltpu.VMEM((3, 2, 80, width), low),
        pltpu.VMEM((4, 48, width), low), pltpu.VMEM((4, 48, width), low),
        pltpu.VMEM((80, width), low), pltpu.VMEM((80, width), low),
    ]
    log_scale, bias = log_scale.reshape(1), bias.reshape(1)
    image_sum, text_sum, scalar_sums = pl.pallas_call(
        kernel,
        out_shape=(grad, grad, jax.ShapeDtypeStruct((8, 128), full)),
        in_specs=[hbm, hbm, hbm, smem, smem],
        out_specs=(vmem,) * 3,
        scratch_shapes=[
            pltpu.VMEM((rows, width), low),
            pltpu.VMEM((rows, width), low),
            pltpu.VMEM((1, images), jnp.int32),
            pltpu.VMEM((images, width), low),
            pltpu.VMEM((texts, width), low),
            pltpu.VMEM((texts, images), low),
            pltpu.VMEM((8, rows, width), low),
            pltpu.VMEM((8, rows, width), low),
            *home,
            *home,
            pltpu.VMEM((3, 8, 128), full),
            pltpu.VMEM((4, 8, 128), full),
            pltpu.VMEM((3, 8, 8, 128), full),
            pltpu.SemaphoreType.DMA((len(NAMES),)),
            pltpu.SemaphoreType.DMA((len(NAMES),)),
            pltpu.SemaphoreType.DMA((3,)),
        ],
        compiler_params=pltpu.CompilerParams(collective_id=0, has_side_effects=True, vmem_limit_bytes=52 * 2**20),
    )(*(pltpu.with_memory_space_constraint(a, pltpu.HBM) for a in (image_emb, text_emb, positive.reshape(1, images))), log_scale, bias)
    loss, image_grad, text_grad, scale_grad, bias_grad = pl.pallas_call(
        project_kernel,
        out_shape=(scalar, grad, grad, scalar, scalar),
        in_specs=[vmem] * 5 + [smem] * 2,
        out_specs=(vmem,) * 5,
        compiler_params=pltpu.CompilerParams(vmem_limit_bytes=16 * 2**20),
    )(image_emb, text_emb, image_sum, text_sum, scalar_sums, log_scale, bias)
    return loss.reshape(()), image_grad, text_grad, scale_grad.reshape(()), bias_grad.reshape(())


def solution(mesh):
    placed = (P(("img", "txt"), None), P(("txt", "img"), None), P("img"), P(), P())
    return jax.shard_map(
        body,
        mesh=mesh,
        in_specs=placed,
        out_specs=(P(), P(("img", "txt"), None), P(("txt", "img"), None), P(), P()),
        check_vma=False,
    )
```

```python
import jax
import jax.numpy as jnp
from jax import lax
from jax.experimental import pallas as pl
from jax.experimental.pallas import tpu as pltpu
from jax.sharding import PartitionSpec as P

EPS = 1e-06
LOG2E = 1.4426950408889634
MESH = pl.DeviceIdType.MESH
OWN, PAIR = 0, 1
ROWS = 128
HALF = ROWS // 2
PLUS, MINUS = 0, 1
PART = ((0, 64), (64, 64))
SPLIT = (((0, 32), (32, 32)), ((64, 32), (96, 32)))
HOME_PART = ((0, 80), (80, 48))
HOME_SPLIT = (((0, 48), (48, 32)), ((80, 16), (96, 32)))
OWN_A, OWN_B, PAIR_A = 0, 1, 2
FIRST = [(OWN, 0), (PAIR, 0), (OWN, 1), (OWN, 3)]
SECOND = [(PAIR, 1), (PAIR, 3), (OWN, 2)]
LAST = [(PAIR, 2)]

NAMES = []
for _kind in ("image", "text"):
    NAMES += [(_kind, "y", h) for h in (0, 1)]
    NAMES += [(_kind, "y_ring", d) for d in (1, 2, 3)]
    NAMES += [(_kind, "own", way, h) for way in (PLUS, MINUS) for h in (0, 1)]
    NAMES += [(_kind, "own2", way, h) for way in (PLUS, MINUS) for h in (0, 1)]
    NAMES += [(_kind, step, way) for step in ("pair", "pair2") for way in (PLUS, MINUS)]
    NAMES += [(_kind, "y_sum", d) for d in range(4)]
    NAMES += [(_kind, step, way, part) for step in ("far", "near") for way in (PLUS, MINUS) for part in range(3)]
    NAMES += [(_kind, "home")]
NAMES += [("core", t, d) for t in (OWN, PAIR) for d in range(4)]
NAMES += [("coresum", t, d) for t in (OWN, PAIR) for d in range(4)]
NAMES += [("sum", "y", d) for d in range(1, 8)]
NAMES += [("sum", axis, d) for axis in ("x", "z") for d in (1, 2, 3)]
IDS = {name: i for i, name in enumerate(NAMES)}


def unit_rows(emb):
    values = emb.astype(jnp.float32)
    norm = jnp.sqrt(jnp.sum(values * values, axis=1, keepdims=True) + EPS)
    return values / norm, norm


PAIRS = 16384


class Ring:
    def __init__(self, kind, rows, partner, plus, minus, slot):
        self.kind, self.rows, self.partner = kind, rows, partner
        self.to = {PLUS: plus, MINUS: minus}
        self.slot = slot

    def part(self, t, d, first, count):
        return self.rows.at[pl.ds(pl.multiple_of(self.slot(t, d) * ROWS + first, 16), count)]


class Home:
    def __init__(self, own, far_out, far_in, near_out, near_in, y_out, y_in, home_out, home_in):
        self.own, self.far_out, self.far_in, self.near_out, self.near_in = own, far_out, far_in, near_out, near_in
        self.y_out, self.y_in, self.home_out, self.home_in = y_out, y_in, home_out, home_in


def kernel(
    image_emb, text_emb, positive_in, log_scale, bias,
    image_sum, text_sum, scalar_sums,
    image_in, text_in, positive, image_rows, text_rows, weight_t, core_out, core_in, *rest,
):
    image_home, text_home = Home(*rest[:9]), Home(*rest[9:18])
    totals, sums, shares, send_sem, recv_sem, load_sem = rest[18:]
    img, txt = lax.axis_index("img"), lax.axis_index("txt")
    z, yh = lax.div(img, 2), lax.rem(img, 2)
    yl, x, c = lax.div(txt, 8), lax.rem(lax.div(txt, 2), 4), lax.rem(txt, 2)

    loads = [
        pltpu.make_async_copy(src, dst, load_sem.at[i])
        for i, (src, dst) in enumerate(((image_emb, image_in), (text_emb, text_in), (positive_in, positive)))
    ]
    for load in loads:
        load.start()

    def device(z=z, yh=yh, yl=yl, x=x, c=c):
        return (z * 2 + yh, yl * 8 + x * 2 + c)

    def step(i, d):
        return lax.rem(i + d, 4)

    def other(bit, t):
        return bit + t * (1 - 2 * bit)

    sibling = device(c=1 - c)
    image_partner = device(yl=1 - yl)
    text_partner = device(yl=1 - yl, yh=1 - yh)
    x_at = {d: device(x=step(x, d)) for d in (1, 2, 3)}
    z_at = {d: device(z=step(z, d)) for d in (1, 2, 3)}

    barrier = pltpu.get_barrier_semaphore()
    y_at = {a * 4 + b * 2 + e: device(yh=other(yh, a), yl=other(yl, b), c=other(c, e)) for a in (0, 1) for b in (0, 1) for e in (0, 1)}
    del y_at[0]
    partners = [*y_at.values(), *x_at.values(), *z_at.values()]
    for partner in partners:
        pl.semaphore_signal(barrier, inc=1, device_id=partner, device_id_type=MESH)

    def image_slot(t, d, core=c):
        return other(yl, t) * 8 + step(x, d) * 2 + core

    def text_slot(t, d):
        return step(z, d) * 2 + other(yh, t)

    image = Ring("image", image_rows, image_partner, x_at[1], x_at[3], image_slot)
    text = Ring("text", text_rows, text_partner, z_at[1], z_at[3], text_slot)

    started = []

    def send(name, src, dst, to):
        i = IDS[name]
        copy = pltpu.make_async_remote_copy(
            src_ref=src, dst_ref=dst, send_sem=send_sem.at[i], recv_sem=recv_sem.at[i], device_id=to, device_id_type=MESH
        )
        copy.start()
        started.append(copy)

    def recv(name, dst):
        i = IDS[name]
        pltpu.make_async_remote_copy(
            src_ref=dst, dst_ref=dst, send_sem=send_sem.at[i], recv_sem=recv_sem.at[i], device_id=sibling, device_id_type=MESH
        ).wait_recv()

    def block(slot):
        return pl.ds(pl.multiple_of(slot * ROWS, ROWS), ROWS)

    def own_rows(load, emb, ring):
        load.wait()
        unit, _ = unit_rows(emb[...])
        ring.rows[block(ring.slot(OWN, 0)), :] = unit.astype(jnp.bfloat16)

    own_rows(loads[0], image_in, image)
    own_rows(loads[1], text_in, text)
    pl.semaphore_wait(barrier, len(partners))

    def forward(ring, name, t, d, first, count, to):
        part = ring.part(t, d, first, count)
        send((ring.kind, *name), part, part, to)

    def arrived(ring, name, t, d, first, count):
        recv((ring.kind, *name), ring.part(t, d, first, count))

    def to_sibling(blocks):
        for t, d in blocks:
            part = image_rows.at[block(image_slot(t, d))]
            send(("core", t, d), part, part, sibling)

    def from_sibling(blocks):
        for t, d in blocks:
            recv(("core", t, d), image_rows.at[block(image_slot(t, d, 1 - c))])

    def near(way):
        return 3 if way == PLUS else 1

    def gather_start(ring):
        forward(ring, ("y", 0), OWN, 0, *PART[0], ring.partner)
        for h in (1, 0):
            for way in (PLUS, MINUS):
                forward(ring, ("own", way, h), OWN, 0, *PART[h], ring.to[way])
        forward(ring, ("y", 1), OWN, 0, *PART[1], ring.partner)

    def gather_ring(ring, h):
        for way in (PLUS, MINUS):
            d = near(way)
            arrived(ring, ("own", way, h), OWN, d, *PART[h])
            forward(ring, ("own2", way, h), OWN, d, *SPLIT[h][way], ring.to[way])
            if h == 1:
                forward(ring, ("y_ring", d), OWN, d, *PART[1], ring.partner)

    def gather_pair(ring):
        arrived(ring, ("y", 0), PAIR, 0, *PART[0])
        for way in (PLUS, MINUS):
            forward(ring, ("pair", way), PAIR, 0, *PART[0], ring.to[way])

    def gather_far(ring):
        for way in (PLUS, MINUS):
            arrived(ring, ("own2", way, 1), OWN, 2, *SPLIT[1][way])
        forward(ring, ("y_ring", 2), OWN, 2, *PART[1], ring.partner)

    def gather_pair_ring(ring):
        for way in (PLUS, MINUS):
            d = near(way)
            arrived(ring, ("pair", way), PAIR, d, *PART[0])
            forward(ring, ("pair2", way), PAIR, d, *SPLIT[0][way], ring.to[way])

    def gather_second(ring):
        for d in (1, 3):
            arrived(ring, ("y_ring", d), PAIR, d, *PART[1])
        for way in (PLUS, MINUS):
            arrived(ring, ("own2", way, 0), OWN, 2, *SPLIT[0][way])

    def gather_last(ring):
        arrived(ring, ("y_ring", 2), PAIR, 2, *PART[1])
        for way in (PLUS, MINUS):
            arrived(ring, ("pair2", way), PAIR, 2, *SPLIT[0][way])

    scale = jnp.exp(jnp.full((1, 256), log_scale[0], jnp.float32))
    scale2 = scale * LOG2E
    bias2 = jnp.full((1, 256), bias[0] * LOG2E, jnp.float32)
    totals[...] = jnp.zeros_like(totals)

    def tile(blocks, t, dx):
        columns = pl.multiple_of(image_slot(t, dx, 0) * ROWS, 256)
        cosine = lax.dot_general(
            jnp.concatenate([text_rows[block(text_slot(*b)), :] for b in blocks], axis=0),
            image_rows[pl.ds(columns, 256), :], (((1,), (1,)), ((), ())), preferred_element_type=jnp.float32,
        )
        wanted = positive[:, pl.ds(columns, 256)]
        add = [jnp.zeros((8, 256), jnp.float32) for _ in range(3)]
        for n, (tt, dz) in enumerate(blocks):
            at = text_slot(tt, dz) * ROWS
            first = ((other(yl, tt) * 8 + x * 2 + c) * 8 + text_slot(tt, dz)) * ROWS
            for part in (0, HALF):
                cos = cosine[n * ROWS + part : n * ROWS + part + HALF]
                row = lax.broadcasted_iota(jnp.int32, (HALF, 256), 0)
                flip = jnp.where(row == wanted - (first + part), -1.0, 1.0)
                e = jnp.exp2((cos * scale2 + bias2) * flip)
                u = 1.0 + e
                w = (e / u) * flip
                weight_t[pl.ds(pl.multiple_of(at + part, HALF), HALF), pl.ds(columns, 256)] = w.astype(jnp.bfloat16)
                e8, u8 = e.reshape(8, 8, 256), u.reshape(8, 8, 256)
                product = e8[0]
                for k in range(1, 8):
                    product = product * u8[k] + e8[k]
                add[0] += jnp.log(1.0 + product)
                add[1] += jnp.sum(w.reshape(8, 8, 256), axis=0)
                add[2] += jnp.sum((w * cos).reshape(8, 8, 256), axis=0)
        for i in range(3):
            totals[i] += add[i][:, :128] + add[i][:, 128:]

    def tiles(blocks, count, place):
        def body(i, carry):
            tile(blocks, *place(i))
            return carry

        lax.fori_loop(0, count, body, 0)

    def first_place(i):
        return lax.rem(i, 2) * (1 - lax.div(i, 2)), lax.div(i * (i - 1), 2)

    def place(t, d):
        return t * 4 + d

    def image_parts(blocks):
        slots = [image_slot(t, d, core) for t, d in blocks for core in (c, 1 - c)]
        lhs = jnp.concatenate([weight_t[:, block(slot)] for slot in slots], axis=1)
        out = lax.dot_general(lhs, text_rows[...], (((0,), (0,)), ((), ())), preferred_element_type=jnp.float32)
        for n, (t, d) in enumerate(blocks):
            core_out[place(t, d)] = out[n * 256 + ROWS : (n + 1) * 256].astype(jnp.bfloat16)
            send(("coresum", t, d), core_out.at[place(t, d)], core_in.at[place(t, d)], sibling)
            image_home.own[place(t, d)] = out[n * 256 : n * 256 + ROWS]

    def text_parts(blocks):
        lhs = jnp.concatenate([weight_t[block(text_slot(t, d)), :] for t, d in blocks], axis=0)
        out = jnp.dot(lhs, image_rows[...], preferred_element_type=jnp.float32)
        for n, (t, d) in enumerate(blocks):
            text_home.own[place(t, d)] = out[n * ROWS : (n + 1) * ROWS]

    def image_ready(blocks):
        for t, d in blocks:
            recv(("coresum", t, d), core_in.at[place(t, d)])

    def rows_of(h):
        return slice(HOME_PART[h][0], sum(HOME_PART[h]))

    def image_part(t, d, h):
        return image_home.own[place(t, d), rows_of(h)] + core_in[place(t, d), rows_of(h)].astype(jnp.float32)

    def text_part(t, d, h):
        return text_home.own[place(t, d), rows_of(h)]

    class Sums:
        def __init__(self, ring, home, part):
            self.ring, self.home, self.part = ring, home, part

        def send(self, name, out, into, to):
            send((self.ring.kind, *name), out, into, to)

        def recv(self, name, into):
            recv((self.ring.kind, *name), into)

        def value(self, part, d):
            if part == OWN_B:
                self.recv(("y_sum", d), self.home.y_in.at[d])
                return self.part(OWN, d, 1) + self.home.y_in[d].astype(jnp.float32)
            return self.part(OWN if part == OWN_A else PAIR, d, 0)

        def send_y(self, d):
            self.home.y_out[d] = self.part(PAIR, d, 1).astype(jnp.bfloat16)
            self.send(("y_sum", d), self.home.y_out.at[d], self.home.y_in.at[d], self.ring.partner)

        def split(self, part, way):
            h = 1 if part == OWN_B else 0
            first, count = HOME_SPLIT[h][way]
            return first - HOME_PART[h][0], count

        def send_far(self, part):
            value = self.value(part, 2).astype(jnp.bfloat16)
            for way in (PLUS, MINUS):
                first, count = self.split(part, way)
                self.home.far_out[part, way, :count] = value[first : first + count]
                out, into = self.home.far_out.at[part, way, pl.ds(0, count)], self.home.far_in.at[part, way, pl.ds(0, count)]
                self.send(("far", way, part), out, into, self.ring.to[way])

        def send_near(self, part):
            for way in (PLUS, MINUS):
                value = self.value(part, 1 if way == PLUS else 3)
                rows = value.shape[0]
                first, count = self.split(part, way)
                out, into = self.home.near_out.at[part, way, pl.ds(0, rows)], self.home.near_in.at[part, way, pl.ds(0, rows)]
                self.recv(("far", way, part), self.home.far_in.at[part, way, pl.ds(0, count)])
                more = self.home.far_in[part, way, :count].astype(jnp.float32)
                for lo, hi in ((0, first), (first, first + count), (first + count, rows)):
                    if lo < hi:
                        piece = value[lo:hi] + more if lo == first else value[lo:hi]
                        self.home.near_out[part, way, lo:hi] = piece.astype(jnp.bfloat16)
                self.send(("near", way, part), out, into, self.ring.to[way])

        def ring_sum(self, part):
            value = self.value(part, 0)
            rows = value.shape[0]
            for way in (PLUS, MINUS):
                self.recv(("near", way, part), self.home.near_in.at[part, way, pl.ds(0, rows)])
                value = value + self.home.near_in[part, way, :rows].astype(jnp.float32)
            return value

        def send_home(self):
            self.home.home_out[...] = self.ring_sum(PAIR_A).astype(jnp.bfloat16)
            self.send(("home",), self.home.home_out, self.home.home_in, self.ring.partner)

        def finish(self, out):
            out[rows_of(1)] = self.ring_sum(OWN_B)
            value = self.ring_sum(OWN_A)
            self.recv(("home",), self.home.home_in)
            out[rows_of(0)] = value + self.home.home_in[...].astype(jnp.float32)

    images, texts = Sums(image, image_home, image_part), Sums(text, text_home, text_part)

    def slot_y(d):
        return other(yh, d // 4) * 4 + other(yl, d // 2 % 2) * 2 + other(c, d % 2)

    stages = {
        "y": (0, 8, slot_y, y_at),
        "x": (1, 4, lambda d: step(x, (4 - d) % 4), x_at),
        "z": (2, 4, lambda d: step(z, (4 - d) % 4), z_at),
    }

    def share(axis):
        i, _, slot, peers = stages[axis]
        shares[i, slot(0)] = sums[i]
        for d, peer in peers.items():
            send(("sum", axis, d), sums.at[i], shares.at[i, slot(0)], peer)

    def shared(axis):
        i, count, slot, peers = stages[axis]
        for d in peers:
            recv(("sum", axis, d), shares.at[i, slot(d)])
        sums[i + 1] = sum(shares[i, k] for k in range(count))

    gather_start(image)
    gather_start(text)
    to_sibling([(OWN, 0)])
    loads[2].wait()
    for ring in (image, text):
        gather_ring(ring, 1)
        gather_pair(ring)
    for ring in (image, text):
        gather_ring(ring, 0)
    for ring in (image, text):
        arrived(ring, ("y", 1), PAIR, 0, *PART[1])
    to_sibling(FIRST[1:])
    gather_far(image)
    gather_far(text)
    from_sibling(FIRST[:2])
    tiles(FIRST, 2, lambda i: (i, 0))
    gather_pair_ring(text)
    gather_pair_ring(image)
    from_sibling(FIRST[2:])
    tiles(FIRST, 2, lambda i: (OWN, 1 + 2 * i))
    gather_second(image)
    to_sibling(SECOND)
    gather_second(text)
    tiles(SECOND, 4, first_place)
    gather_last(image)
    to_sibling(LAST)
    gather_last(text)
    every = FIRST + SECOND + LAST
    gathered = len(started)
    from_sibling(SECOND)
    tile(every, OWN, 2)
    from_sibling(LAST)
    tile(every, PAIR, 2)
    image_parts([(PAIR, 2), (OWN, 2)])
    tiles(every, 2, lambda i: (PAIR, 1 + 2 * i))
    image_ready([(PAIR, 2), (OWN, 2)])
    images.send_y(2)
    images.send_far(PAIR_A)
    images.send_far(OWN_A)
    for t, d in FIRST:
        tile(LAST, t, d)
    for i in range(3):
        sums[0, i : i + 1] = jnp.sum(totals[i], axis=0, keepdims=True)
    sums[0, 3:] = jnp.zeros((5, 128), jnp.float32)
    share("y")
    text_parts([(PAIR, 2), (OWN, 2)])
    texts.send_y(2)
    texts.send_far(PAIR_A)
    texts.send_far(OWN_A)
    image_parts([(PAIR, 1), (PAIR, 3)])
    shared("y")
    share("x")
    text_parts([(PAIR, 1), (PAIR, 3)])
    texts.send_y(1)
    texts.send_y(3)
    image_ready([(PAIR, 1), (PAIR, 3)])
    images.send_y(1)
    images.send_y(3)
    images.send_near(PAIR_A)
    texts.send_near(PAIR_A)
    images.send_far(OWN_B)
    image_parts([(OWN, 1), (OWN, 3)])
    shared("x")
    share("z")
    texts.send_far(OWN_B)
    image_parts([(PAIR, 0)])
    text_parts([(PAIR, 0)])
    texts.send_y(0)
    text_parts([(OWN, 1), (OWN, 3)])
    image_ready([(OWN, 1), (OWN, 3)])
    images.send_near(OWN_A)
    texts.send_near(OWN_A)
    image_ready([(PAIR, 0)])
    images.send_y(0)
    images.send_home()
    texts.send_home()
    images.send_near(OWN_B)
    texts.send_near(OWN_B)
    for copy in started[:gathered]:
        copy.wait_send()
    image_parts([(OWN, 0)])
    text_parts([(OWN, 0)])
    for copy in started[gathered:]:
        copy.wait_send()
    shared("z")
    scalar_sums[...] = sums[3]
    image_ready([(OWN, 0)])
    images.finish(image_sum)
    texts.finish(text_sum)


def project_kernel(
    image_emb, text_emb, image_sum, text_sum, scalar_sums, log_scale, bias, loss, image_grad, text_grad, scale_grad, bias_grad
):
    scale = jnp.exp(jnp.full((1, 1), log_scale[0], jnp.float32))
    for emb, summed, grad in ((image_emb, image_sum, image_grad), (text_emb, text_sum, text_grad)):
        unit, norm = unit_rows(emb[...])
        value = summed[...] * scale
        grad[...] = (value - unit * jnp.sum(unit * value, axis=1, keepdims=True)) / norm
    total = jnp.sum(scalar_sums[...], axis=1, keepdims=True)
    loss[...] = total[0:1] / PAIRS
    bias_grad[...] = total[1:2]
    scale_grad[...] = scale * total[2:3]


def body(image_emb, text_emb, positive, log_scale, bias):
    rows, width = image_emb.shape
    images, texts = 16 * rows, 8 * rows
    low, full = jnp.bfloat16, jnp.float32
    vmem = pl.BlockSpec(memory_space=pltpu.VMEM)
    smem = pl.BlockSpec(memory_space=pltpu.SMEM)
    hbm = pl.BlockSpec(memory_space=pl.ANY)
    scalar = jax.ShapeDtypeStruct((1, 1), full)
    grad = jax.ShapeDtypeStruct((rows, width), full)
    home = [
        pltpu.VMEM((8, rows, width), full),
        pltpu.VMEM((3, 2, 48, width), low), pltpu.VMEM((3, 2, 48, width), low),
        pltpu.VMEM((3, 2, 80, width), low), pltpu.VMEM((3, 2, 80, width), low),
        pltpu.VMEM((4, 48, width), low), pltpu.VMEM((4, 48, width), low),
        pltpu.VMEM((80, width), low), pltpu.VMEM((80, width), low),
    ]
    log_scale, bias = log_scale.reshape(1), bias.reshape(1)
    image_sum, text_sum, scalar_sums = pl.pallas_call(
        kernel,
        out_shape=(grad, grad, jax.ShapeDtypeStruct((8, 128), full)),
        in_specs=[hbm, hbm, hbm, smem, smem],
        out_specs=(vmem,) * 3,
        scratch_shapes=[
            pltpu.VMEM((rows, width), low),
            pltpu.VMEM((rows, width), low),
            pltpu.VMEM((1, images), jnp.int32),
            pltpu.VMEM((images, width), low),
            pltpu.VMEM((texts, width), low),
            pltpu.VMEM((texts, images), low),
            pltpu.VMEM((8, rows, width), low),
            pltpu.VMEM((8, rows, width), low),
            *home,
            *home,
            pltpu.VMEM((3, 8, 128), full),
            pltpu.VMEM((4, 8, 128), full),
            pltpu.VMEM((3, 8, 8, 128), full),
            pltpu.SemaphoreType.DMA((len(NAMES),)),
            pltpu.SemaphoreType.DMA((len(NAMES),)),
            pltpu.SemaphoreType.DMA((3,)),
        ],
        compiler_params=pltpu.CompilerParams(collective_id=0, has_side_effects=True, vmem_limit_bytes=52 * 2**20),
    )(*(pltpu.with_memory_space_constraint(a, pltpu.HBM) for a in (image_emb, text_emb, positive.reshape(1, images))), log_scale, bias)
    loss, image_grad, text_grad, scale_grad, bias_grad = pl.pallas_call(
        project_kernel,
        out_shape=(scalar, grad, grad, scalar, scalar),
        in_specs=[vmem] * 5 + [smem] * 2,
        out_specs=(vmem,) * 5,
        compiler_params=pltpu.CompilerParams(vmem_limit_bytes=16 * 2**20),
    )(image_emb, text_emb, image_sum, text_sum, scalar_sums, log_scale, bias)
    return loss.reshape(()), image_grad, text_grad, scale_grad.reshape(()), bias_grad.reshape(())


def solution(mesh):
    placed = (P(("img", "txt"), None), P(("txt", "img"), None), P("img"), P(), P())
    return jax.shard_map(
        body,
        mesh=mesh,
        in_specs=placed,
        out_specs=(P(), P(("img", "txt"), None), P(("txt", "img"), None), P(), P()),
        check_vma=False,
    )
```
